128 devices in a mesh: dp: 32 (over z, y, core), tp: 4 (over x).
Axes of the slice: x: 4, y: 4, z: 4, core: 2. Of those that a mesh axis runs over, the one named last changes fastest.
Arguments:
- queries: bfloat16 [4096, 36864], P('dp', 'tp'), may hold values from -32 to 32
- latents: bfloat16 [4096, 576], P(('dp', 'tp')), may hold values from -32 to 32
- segment_ids: int32 [4096], P('dp'), may hold values from 0 to 3, never falling along the last dimension, each value on 1 to 2048 neighbouring positions
- value_weight: bfloat16 [64, 512, 128], P('tp', 'dp'), may hold values from -0.25 to 0.25
Outputs:
- attended: bfloat16 [4096, 8192], P('dp', 'tp')
The draws below stay inside these ranges and needn't reach their ends.
Inputs may be any that keep to these rules, and one draw needn't show every extreme that they name: `segment_ids`: ids never fall along the pack; each document holds 1 to 2048 tokens and one holds exactly 2048.
All inputs are finite; a program needn't handle non-finite values.
Results may differ from the reference program's by a relative error of at most 0.0055.
Values may be sent and summed in bfloat16 or wider, within the bound.
A program may use at most 192 MiB of HBM per device.

```python
import math
import jax
import jax.numpy as jnp
import numpy as np
from jax import lax

HEADS = 64
LATENT = 512
ROPE = 64
VALUE = 128
TOK_DEV = 128
DOCS = 4
TOKENS = 4096
MOST = 2048


def base_latents(key):
    rough = jax.random.normal(jax.random.fold_in(key, 101), (TOKENS, LATENT + ROPE), jnp.float32)
    offsets = jax.random.normal(jax.random.fold_in(key, 103), (TOKENS // TOK_DEV, LATENT + ROPE), jnp.float32)
    feature_mask = (jnp.arange(LATENT + ROPE) < LATENT).astype(jnp.float32)
    offsets = offsets * feature_mask[None, :]
    return rough + jnp.repeat(offsets, TOK_DEV, axis=0)


def draw_latents(key, part):
    base = base_latents(key)
    return jnp.clip(base, -32.0, 32.0).astype(jnp.bfloat16)


def draw_queries(key, part):
    key = jax.random.fold_in(key, 2)
    fresh = jax.random.normal(key, (TOKENS, HEADS, LATENT + ROPE), jnp.float32)
    return jnp.clip(fresh, -32.0, 32.0).reshape(TOKENS, HEADS * (LATENT + ROPE)).astype(jnp.bfloat16)


def block_levels(key, shape, shards, least, top_value):
    gain = 1.0
    for position, parts in shards:
        steps = jax.random.uniform(jax.random.fold_in(jax.random.fold_in(key, 6), position), (parts,), jnp.float32, least / len(shards), top_value / len(shards))
        gain = gain * jnp.repeat(jnp.exp(steps), shape[position] // parts).reshape((-1,) + (1,) * (len(shape) - 1 - position))
    return gain


def length_profile(count, total, bound, skew):
    portions = [(1 << 20) // math.isqrt(standing ** skew) + 1 for standing in range(2, count + 1)]
    rest, holding = total - bound - (count - 1), [1] * (count - 1)
    while rest > 0:
        candidates = [i for i in range(count - 1) if holding[i] < bound]
        whole, budget = sum([portions[i] for i in candidates]), rest
        for i in candidates:
            addition = min(bound - holding[i], max(1, budget * portions[i] // whole), rest)
            holding[i] = holding[i] + addition
            rest = rest - addition
    return np.array([bound] + holding)


def ragged_sizes(key, number_of, total, most, lean):
    if number_of == 2:
        one = jax.random.randint(key, (), max(1, total - most), min(most, total - 1) + 1)
        return jnp.stack([one, total - one])
    tallies = jnp.asarray(length_profile(number_of, total, most, lean), jnp.int32)
    pairs = (number_of - 1) // 2
    donor, sink = tallies[1:1 + 2 * pairs:2], tallies[2:2 + 2 * pairs:2]
    margin = jnp.minimum(donor - 1, most - sink)
    passed = jax.random.randint(jax.random.fold_in(key, 1), (pairs,), 0, 1 << 20) % (margin + 1)
    tallies = tallies.at[1:1 + 2 * pairs:2].set(donor - passed).at[2:2 + 2 * pairs:2].set(sink + passed)
    return tallies[jax.random.permutation(jax.random.fold_in(key, 2), number_of)]


def bell_draw(rng, extent, width, most, cuts=(), held_as=jnp.bfloat16):
    result = width * jax.random.normal(rng, extent, jnp.float32)
    if cuts:
        result = result * block_levels(rng, extent, cuts, -0.22, 0.18)
    return jnp.clip(result, -most, most).astype(held_as)


def setup_inputs(seed: int = 0) -> dict:
    key_of = jax.random.split(jax.random.key(seed), 5)
    return {
        "queries": draw_queries(jax.random.fold_in(key_of[4], 71), 0),
        "latents": draw_latents(jax.random.fold_in(key_of[4], 71), 0),
        "segment_ids": jnp.searchsorted(jnp.cumsum(ragged_sizes(key_of[2], DOCS, TOKENS, MOST, 2)), jnp.arange(TOKENS), side="right").astype(jnp.int32),
        "value_weight": bell_draw(key_of[3], (HEADS, LATENT, VALUE), LATENT ** -0.5, 0.25, ((0, 4), (1, 32))),
    }


score_scale = 192.0 ** -0.5
masked_value = -1.0e30


def reference(queries, latents, segment_ids, value_weight):
    feature_width = LATENT + ROPE
    query_all = queries.reshape(TOKENS, HEADS, feature_width)
    padded_keys = jnp.concatenate([jnp.zeros((MOST, feature_width), jnp.bfloat16), latents], 0)
    padded_ids = jnp.concatenate([jnp.full((MOST,), -1, jnp.int32), segment_ids], 0)

    def one_block(index):
        anchor = (index * TOK_DEV).astype(jnp.int32)
        query_rows = lax.dynamic_slice_in_dim(query_all, anchor, TOK_DEV, 0).astype(jnp.float32)
        query_ids = lax.dynamic_slice_in_dim(segment_ids, anchor, TOK_DEV, 0)
        key_rows = lax.dynamic_slice_in_dim(padded_keys, anchor, MOST + TOK_DEV, 0)
        key_ids = lax.dynamic_slice_in_dim(padded_ids, anchor, MOST + TOK_DEV, 0)
        query_position = anchor + jnp.arange(TOK_DEV, dtype=jnp.int32)
        key_position = anchor - MOST + jnp.arange(MOST + TOK_DEV, dtype=jnp.int32)
        allowed = (query_ids[:, None] == key_ids[None, :]) & (key_position[None, :] <= query_position[:, None])
        scores = jnp.einsum('thd,kd->thk', query_rows, key_rows.astype(jnp.float32)) * score_scale
        scores = jnp.where(allowed[:, None, :], scores, masked_value)
        highest = jnp.max(scores, axis=2, keepdims=True)
        weights = jnp.where(allowed[:, None, :], jnp.exp(scores - highest), 0.0)
        weight_sum = jnp.sum(weights, axis=2)
        rounded = lax.optimization_barrier(weights.astype(jnp.bfloat16)).astype(jnp.float32)
        context = jnp.einsum('thk,kc->thc', rounded, key_rows[:, :LATENT].astype(jnp.float32)) / weight_sum[..., None]
        context = lax.optimization_barrier(context.astype(jnp.bfloat16)).astype(jnp.float32)
        projected = jnp.einsum('thc,hcv->thv', context, value_weight.astype(jnp.float32))
        return projected.astype(jnp.bfloat16).reshape(TOK_DEV, HEADS * VALUE)

    blocks = lax.map(one_block, jnp.arange(TOKENS // TOK_DEV, dtype=jnp.int32))
    return blocks.reshape(TOKENS, HEADS * VALUE)
```

```python
import functools

import jax
import jax.numpy as jnp
from jax import lax
from jax.experimental import pallas as pl
from jax.experimental.pallas import tpu as pltpu
from jax.sharding import PartitionSpec as P

MESH = pl.DeviceIdType.MESH
F32, BF16 = jnp.float32, jnp.bfloat16
LATENT, ROPE, VALUE = 512, 64, 128
FEAT = LATENT + ROPE
WIDE = 640
TOK = 128
HEADS = 16
ROWS = TOK * HEADS
CHUNK = 2 * TOK
NCH = 9
SHARD = 32
GROUPS = ((0, 1, 4, 2), (3, 5, 6, 7, 8))
FULL = (1, 4)
QUARTER = (2, 3, 5, 6, 7, 8)
R2 = 512
C = 192.0 ** -0.5 * 1.4426950408889634
BIG = -1.0e30
NT = (((1,), (1,)), ((), ()))


def kernel(q_hbm, lat_ref, seg_ref, w_hbm, o_ref,
           kbuf, wbuf, qv, qs, segc, S, mx, p0, p1, l0, l1, lsum, mold, acc, ctx,
           q_sem, w_sem, sx, rx, sb, rb, ss, rs, swy, rwy, swz, rwz, sws, rws):
    dp, tp = lax.axis_index("dp"), lax.axis_index("tp")
    core = lax.rem(dp, 2)
    y = lax.rem(dp // 2, 4)
    z = dp // 8
    sib = dp + 1 - 2 * core

    def xpeer(d):
        return (dp, lax.rem(tp + d, 4))

    def ypeer(d):
        return (z * 8 + lax.rem(y + d, 4) * 2 + core, tp)

    def zpeer(d):
        return (lax.rem(z + d, 4) * 8 + y * 2 + core, tp)

    def has_dst(k):
        return dp + 2 * k <= 31

    def has_src(k):
        return dp - 2 * k >= 0

    qcopy = [pltpu.make_async_copy(q_hbm.at[:, pl.ds(g * 2 * FEAT, 2 * FEAT)], qv.at[g], q_sem.at[g]) for g in range(HEADS // 2)]
    for cp in qcopy:
        cp.start()
    wown = pltpu.make_async_copy(w_hbm, wbuf.at[:, z, y, core], w_sem.at[0])
    wown.start()

    barrier = pltpu.get_barrier_semaphore()

    def greet(dev):
        pl.semaphore_signal(barrier, inc=1, device_id=dev, device_id_type=MESH)

    for d in range(1, 4):
        greet(xpeer(d))
        greet(ypeer(d))
        greet(zpeer(d))
    greet((sib, tp))
    for k in range(1, NCH):
        @pl.when(has_src(k))
        def _():
            greet((dp - 2 * k, tp))

    seg = jnp.broadcast_to(seg_ref[...].astype(F32), (TOK, TOK))
    segc[...] = jnp.transpose(seg)
    my_rows = pl.ds(pl.multiple_of(core * TOK + tp * SHARD, SHARD), SHARD)
    half = pl.ds(pl.multiple_of(core * TOK, TOK), TOK)
    other = pl.ds(pl.multiple_of((1 - core) * TOK, TOK), TOK)
    lane32 = lax.broadcasted_iota(jnp.int32, (SHARD, 128), 1).astype(F32)
    mine = segc[pl.ds(pl.multiple_of(tp * SHARD, SHARD), SHARD), :]
    kfeat = jnp.where((lane32 >= 4.0) | (lane32 == mine), 0.0, BIG).astype(BF16)
    kbuf[0, my_rows, 0:FEAT] = lat_ref[...]
    kbuf[0, my_rows, FEAT:WIDE] = kfeat[:, :WIDE - FEAT]

    n_wait = 10 + jnp.minimum(NCH - 1, 15 - dp // 2)
    pl.semaphore_wait(barrier, n_wait)

    def xcopy(k, d):
        return pltpu.make_async_remote_copy(kbuf.at[k, my_rows, :], kbuf.at[k, my_rows, :], sx.at[k, d], rx.at[k, d], device_id=xpeer(d), device_id_type=MESH)

    def bcopy(k):
        rows = half if k in FULL else my_rows
        return pltpu.make_async_remote_copy(kbuf.at[0, rows, :], kbuf.at[k, rows, :], sb.at[k], rb.at[k], device_id=(dp + 2 * k, tp), device_id_type=MESH)

    def scopy(k):
        return pltpu.make_async_remote_copy(kbuf.at[k, half, :], kbuf.at[k, half, :], ss.at[k], rs.at[k], device_id=(sib, tp), device_id_type=MESH)

    for d in (1, 3, 2):
        xcopy(0, d).start()
    for k in QUARTER:
        @pl.when(has_dst(k))
        def _():
            bcopy(k).start()

    def wcopy(ref_src, where, ssem, rsem, dev):
        return pltpu.make_async_remote_copy(ref_src, where, ssem, rsem, device_id=dev, device_id_type=MESH)

    H2 = HEADS // 2
    lo, hi = pl.ds(0, H2), pl.ds(H2, H2)

    def wy1(d):
        return wcopy(w_hbm.at[lo], wbuf.at[lo, z, y, core], swy.at[0, d], rwy.at[0, d], ypeer(d))

    def wz1(d):
        return wcopy(w_hbm.at[hi], wbuf.at[hi, z, y, core], swz.at[0, d], rwz.at[0, d], zpeer(d))

    def wz2(d):
        return wcopy(wbuf.at[lo, z, :, core], wbuf.at[lo, z, :, core], swz.at[1, d], rwz.at[1, d], zpeer(d))

    def wy2(d):
        return wcopy(wbuf.at[hi, :, y, core], wbuf.at[hi, :, y, core], swy.at[1, d], rwy.at[1, d], ypeer(d))

    def wsib():
        return wcopy(wbuf.at[:, :, :, core], wbuf.at[:, :, :, core], sws.at[0], rws.at[0], (sib, tp))

    segv = segc[...]
    lane = lax.broadcasted_iota(jnp.int32, (TOK, 128), 1)
    onehot = jnp.where((lane - 64).astype(F32) == segv, 1.0, 0.0)

    def prep(g):
        qcopy[g].wait()
        even = qv[g, :, 0:WIDE]
        odd = pltpu.roll(qv[g, :, LATENT:2 * FEAT], WIDE - 64, 1)
        for i, v in ((0, even), (1, odd)):
            r = pl.ds((2 * g + i) * TOK, TOK)
            qs[r, 0:LATENT] = v[:, 0:LATENT]
            qs[r, LATENT:WIDE] = jnp.where(lane < 64, v[:, LATENT:WIDE].astype(F32), onehot).astype(BF16)

    for g in range(HEADS // 2):
        prep(g)

    for k in range(1, NCH):
        @pl.when(jnp.logical_not(has_src(k)))
        def _():
            ln = lax.broadcasted_iota(jnp.int32, (CHUNK, 128), 1)
            kbuf[k, :, 0:LATENT] = jnp.zeros((CHUNK, LATENT), BF16)
            kbuf[k, :, LATENT:WIDE] = jnp.where((ln >= 64) & (ln < 68), BIG, 0.0).astype(BF16)

    for d in range(1, 4):
        xcopy(0, d).wait_recv()
    scopy(0).start()
    for k in FULL:
        @pl.when(has_dst(k))
        def _():
            bcopy(k).start()
    for k in QUARTER:
        @pl.when(has_src(k))
        def _():
            bcopy(k).wait_recv()
            for d in (1, 3, 2):
                xcopy(k, d).start()
    for d in (1, 3, 2):
        wy1(d).start()
        wz1(d).start()

    def relay(k):
        @pl.when(has_src(k))
        def _():
            if k in FULL:
                bcopy(k).wait_recv()
            else:
                for d in range(1, 4):
                    xcopy(k, d).wait_recv()
            scopy(k).start()

    def arrive(k):
        if k == 0:
            scopy(0).wait_recv()
        else:
            @pl.when(has_src(k))
            def _():
                scopy(k).wait_recv()

    def score(k, slot, first):
        s = lax.dot_general(qs[...], kbuf[k], NT, preferred_element_type=F32)
        if k == 0:
            rr = lax.broadcasted_iota(jnp.int32, (ROWS, CHUNK), 0)
            cc = lax.broadcasted_iota(jnp.int32, (ROWS, CHUNK), 1)
            s = jnp.where(cc <= (rr & (TOK - 1)) + core * TOK, s, BIG)
        S[slot] = s
        m = jnp.maximum(s[:, :128], s[:, 128:])
        mx[...] = m if first else jnp.maximum(mx[...], m)

    ps, ls = (p0, p1), (l0, l1)

    def weigh(gi, r):
        rows = pl.ds(r * R2, R2)
        m = jnp.max(mx[rows, :], axis=1, keepdims=True) * C
        n = len(GROUPS[gi])
        l = None
        for j in range(n):
            p = jnp.exp2(S[j, rows, :] * C - m)
            t = p[:, :128] + p[:, 128:]
            l = t if l is None else l + t
            ps[r % 2][:, j * CHUNK:(j + 1) * CHUNK] = p.astype(BF16)
        ls[r % 2][...] = l
        return m

    def gather_values(gi):
        ks = GROUPS[gi]
        return jnp.concatenate([kbuf[k, :, 0:LATENT] for k in ks], axis=0)

    def values(gi, r, m):
        rows = pl.ds(r * R2, R2)
        n = len(GROUPS[gi])
        a = jnp.dot(ps[r % 2][:, 0:n * CHUNK], gather_values(gi), preferred_element_type=F32)
        l = ls[r % 2][...]
        last = gi == len(GROUPS) - 1
        if gi > 0:
            al = jnp.exp2(mold[rows, 0:1] - m)
            a = a + acc[rows, :] * al
            l = l + lsum[rows, :] * al
        if last:
            inv = 1.0 / jnp.sum(l, axis=1, keepdims=True)
            ctx[rows, :] = (a * inv).astype(BF16)
        else:
            acc[rows, :] = a
            lsum[rows, :] = l
            mold[rows, :] = jnp.broadcast_to(m, (R2, 128))

    order = [k for g in GROUPS for k in g]
    relay(order[1])
    pos = 0
    for gi, ks in enumerate(GROUPS):
        for slot, k in enumerate(ks):
            arrive(k)
            score(k, slot, pos == 0)
            pos += 1
            if pos + 1 < NCH:
                relay(order[pos + 1])
            if pos == 3:
                for d in range(1, 4):
                    wy1(d).wait_recv()
                    wz1(d).wait_recv()
                wown.wait()
                for d in (1, 3, 2):
                    wz2(d).start()
                    wy2(d).start()
        if gi == len(GROUPS) - 1:
            for d in range(1, 4):
                wz2(d).wait_recv()
                wy2(d).wait_recv()
            wsib().start()
        n = ROWS // R2
        m = weigh(gi, 0)
        for r in range(n):
            nm = weigh(gi, r + 1) if r + 1 < n else None
            values(gi, r, m)
            m = nm

    wsib().wait_recv()
    for h in range(HEADS):
        wv = wbuf[h].reshape(LATENT, VALUE)
        o_ref[:, h * VALUE:(h + 1) * VALUE] = jnp.dot(ctx[h * TOK:(h + 1) * TOK, :], wv, preferred_element_type=F32).astype(BF16)

    for d in range(1, 4):
        xcopy(0, d).wait_send()
        wy1(d).wait_send()
        wz1(d).wait_send()
        wy2(d).wait_send()
        wz2(d).wait_send()
    scopy(0).wait_send()
    wsib().wait_send()
    for k in range(1, NCH):
        @pl.when(has_dst(k))
        def _():
            bcopy(k).wait_send()

        @pl.when(has_src(k))
        def _():
            scopy(k).wait_send()
            if k in QUARTER:
                for d in range(1, 4):
                    xcopy(k, d).wait_send()


def per_device(queries, latents, segment_ids, value_weight):
    dma = pltpu.SemaphoreType.DMA
    gmax = max(len(g) for g in GROUPS)
    return pl.pallas_call(
        kernel,
        out_shape=jax.ShapeDtypeStruct((TOK, HEADS * VALUE), BF16),
        in_specs=[pl.BlockSpec(memory_space=pl.ANY), pl.BlockSpec(memory_space=pltpu.VMEM), pl.BlockSpec(memory_space=pltpu.VMEM), pl.BlockSpec(memory_space=pl.ANY)],
        out_specs=pl.BlockSpec(memory_space=pltpu.VMEM),
        scratch_shapes=[
            pltpu.VMEM((NCH, CHUNK, WIDE), BF16),
            pltpu.VMEM((HEADS, 4, 4, 2, 16, VALUE), BF16),
            pltpu.VMEM((HEADS // 2, TOK, 2 * FEAT), BF16),
            pltpu.VMEM((ROWS, WIDE), BF16),
            pltpu.VMEM((TOK, 128), F32),
            pltpu.VMEM((gmax, ROWS, CHUNK), F32),
            pltpu.VMEM((ROWS, 128), F32),
            pltpu.VMEM((R2, gmax * CHUNK), BF16),
            pltpu.VMEM((R2, gmax * CHUNK), BF16),
            pltpu.VMEM((R2, 128), F32),
            pltpu.VMEM((R2, 128), F32),
            pltpu.VMEM((ROWS, 128), F32),
            pltpu.VMEM((ROWS, 128), F32),
            pltpu.VMEM((ROWS, LATENT), F32),
            pltpu.VMEM((ROWS, LATENT), BF16),
            dma((HEADS // 2,)), dma((1,)),
            dma((NCH, 4)), dma((NCH, 4)),
            dma((NCH,)), dma((NCH,)),
            dma((NCH,)), dma((NCH,)),
            dma((2, 4)), dma((2, 4)),
            dma((2, 4)), dma((2, 4)),
            dma((1,)), dma((1,)),
        ],
        compiler_params=pltpu.CompilerParams(collective_id=0, has_side_effects=True, vmem_limit_bytes=56 * 2 ** 20),
        cost_estimate=pl.CostEstimate(flops=11 * 10 ** 9, bytes_accessed=8 * 10 ** 6, transcendentals=5 * 10 ** 6),
    )(queries, latents, segment_ids.reshape(1, TOK), value_weight)


def solution(mesh):
    placed = (P("dp", "tp"), P(("dp", "tp"), None), P("dp"), P("tp", "dp", None))
    return jax.shard_map(per_device, mesh=mesh, in_specs=placed, out_specs=P("dp", "tp"), check_vma=False)
```

```python
import functools

import jax
import jax.numpy as jnp
from jax import lax
from jax.experimental import pallas as pl
from jax.experimental.pallas import tpu as pltpu
from jax.sharding import PartitionSpec as P

MESH = pl.DeviceIdType.MESH
F32, BF16 = jnp.float32, jnp.bfloat16
LATENT, ROPE, VALUE = 512, 64, 128
FEAT = LATENT + ROPE
WIDE = 640
TOK = 128
HEADS = 16
ROWS = TOK * HEADS
CHUNK = 2 * TOK
NCH = 9
SHARD = 32
GROUPS = ((0, 4, 1, 3), (8, 2, 6, 5, 7))
DIRECT = (1, 3)
ALONG = (5, 7)
SHARDS = (1, 3, 2, 6, 5, 7)
R1 = 512
R2 = 512
C = 192.0 ** -0.5 * 1.4426950408889634
BIG = -1.0e30
NT = (((1,), (1,)), ((), ()))


def kernel(q_hbm, lat_ref, seg_ref, w_hbm, o_ref,
           kbuf, wbuf, qv, qs, segc, S, mx, p0, p1, l0, l1, lsum, mold, acc, ctx,
           q_sem, w_sem, sx, rx, sb, sy, ry, sz, rz, ss, rs, swy, rwy, swz, rwz, sws, rws):
    dp, tp = lax.axis_index("dp"), lax.axis_index("tp")
    core = lax.rem(dp, 2)
    y = lax.rem(dp // 2, 4)
    z = dp // 8
    sib = dp + 1 - 2 * core

    def xpeer(d):
        return (dp, lax.rem(tp + d, 4))

    def ypeer(d):
        return (z * 8 + lax.rem(y + d, 4) * 2 + core, tp)

    def zpeer(d):
        return (lax.rem(z + d, 4) * 8 + y * 2 + core, tp)

    def has_src(k):
        return dp - 2 * k >= 0

    qcopy = [pltpu.make_async_copy(q_hbm.at[:, pl.ds(g * 2 * FEAT, 2 * FEAT)], qv.at[g], q_sem.at[g]) for g in range(HEADS // 2)]
    for cp in qcopy:
        cp.start()
    wown = pltpu.make_async_copy(w_hbm, wbuf.at[:, z, y, core], w_sem.at[0])
    wown.start()

    barrier = pltpu.get_barrier_semaphore()

    def greet(dev):
        pl.semaphore_signal(barrier, inc=1, device_id=dev, device_id_type=MESH)

    for d in range(1, 4):
        greet(xpeer(d))
        greet(ypeer(d))
        greet(zpeer(d))
    greet((sib, tp))
    for k in DIRECT:
        @pl.when((core == 0) & has_src(k))
        def _():
            greet((dp - 2 * k, tp))

    seg = jnp.broadcast_to(seg_ref[...].astype(F32), (TOK, TOK))
    segc[...] = jnp.transpose(seg)
    my_rows = pl.ds(pl.multiple_of(core * TOK + tp * SHARD, SHARD), SHARD)
    half = pl.ds(pl.multiple_of(core * TOK, TOK), TOK)
    other = pl.ds(pl.multiple_of((1 - core) * TOK, TOK), TOK)
    lane32 = lax.broadcasted_iota(jnp.int32, (SHARD, 128), 1).astype(F32)
    mine = segc[pl.ds(pl.multiple_of(tp * SHARD, SHARD), SHARD), :]
    kfeat = jnp.where((lane32 >= 4.0) | (lane32 == mine), 0.0, BIG).astype(BF16)
    kbuf[0, my_rows, 0:FEAT] = lat_ref[...]
    kbuf[0, my_rows, FEAT:WIDE] = kfeat[:, :WIDE - FEAT]

    n_wait = 10 + jnp.where(core == 0, jnp.where(dp + 2 <= 31, 1, 0) + jnp.where(dp + 6 <= 31, 1, 0), 0)
    pl.semaphore_wait(barrier, n_wait)

    def remote(ref, dst, ssem, rsem, dev):
        return pltpu.make_async_remote_copy(ref, dst, ssem, rsem, device_id=dev, device_id_type=MESH)

    def zdev(v):
        return (v * 8 + y * 2 + core, tp)

    def xcopy(k, d):
        at = kbuf.at[k, my_rows, :]
        return remote(at, at, sx.at[k, d], rx.at[k, d], xpeer(d))

    def zcopy(r):
        return remote(kbuf.at[0, my_rows, :], kbuf.at[4 * r, my_rows, :], sz.at[r], rz.at[r], zdev(lax.rem(z + r, 4)))

    first = core == 0
    second = core == 1

    def yrow(k):
        return k // 4 + jnp.where(y + k % 4 <= 3, 0, 1)

    def ycopy(k, rows):
        return remote(kbuf.at[4 * yrow(k), rows, :], kbuf.at[k, rows, :], sy.at[k], ry.at[k], ypeer(k % 4))

    def yneed(k):
        return z >= yrow(k)

    def bcopy(k):
        return remote(kbuf.at[0, half, :], kbuf.at[k, half, :], sb.at[k], ry.at[k], (dp + 2 * k, tp))

    def scopy(k):
        at = kbuf.at[k, half, :]
        return remote(at, at, ss.at[k], rs.at[k], (sib, tp))

    H2 = HEADS // 2

    lo, hi = pl.ds(0, H2), pl.ds(H2, H2)

    def wy1(d):
        return remote(w_hbm.at[lo], wbuf.at[lo, z, y, core], swy.at[0, d], rwy.at[0, d], ypeer(d))

    def wz1(d):
        return remote(w_hbm.at[hi], wbuf.at[hi, z, y, core], swz.at[0, d], rwz.at[0, d], zpeer(d))

    def wz2(d):
        at = wbuf.at[lo, z, :, core]
        return remote(at, at, swz.at[1, d], rwz.at[1, d], zpeer(d))

    def wy2(d):
        at = wbuf.at[hi, :, y, core]
        return remote(at, at, swy.at[1, d], rwy.at[1, d], ypeer(d))

    def wsib(i):
        at = wbuf.at[(lo, hi)[i], :, :, core]
        return remote(at, at, sws.at[i], rws.at[i], (sib, tp))

    def shards(k):
        return second if k in DIRECT + ALONG else True

    for r in (1, 2):
        @pl.when(z + r <= 3)
        def _():
            zcopy(r).start()
    for d in (1, 3, 2):
        xcopy(0, d).start()
    for k in SHARDS:
        @pl.when((yrow(k) == 0) & shards(k))
        def _():
            ycopy(k, my_rows).start()

    segv = segc[...]
    lane = lax.broadcasted_iota(jnp.int32, (TOK, 128), 1)
    onehot = jnp.where((lane - 64).astype(F32) == segv, 1.0, 0.0)

    def prep(g):
        qcopy[g].wait()
        even = qv[g, :, 0:WIDE]
        odd = pltpu.roll(qv[g, :, LATENT:2 * FEAT], WIDE - 64, 1)
        for i, v in ((0, even), (1, odd)):
            r = pl.ds((2 * g + i) * TOK, TOK)
            qs[r, 0:LATENT] = v[:, 0:LATENT]
            qs[r, LATENT:WIDE] = jnp.where(lane < 64, v[:, LATENT:WIDE].astype(F32), onehot).astype(BF16)

    for k in range(1, NCH):
        @pl.when(jnp.logical_not(has_src(k)))
        def _():
            ln = lax.broadcasted_iota(jnp.int32, (CHUNK, 128), 1)
            kbuf[k, :, 0:LATENT] = jnp.zeros((CHUNK, LATENT), BF16)
            kbuf[k, :, LATENT:WIDE] = jnp.where((ln >= 64) & (ln < 68), BIG, 0.0).astype(BF16)

    for g in range(HEADS // 2):
        prep(g)

    for r in (1, 2):
        @pl.when(z >= r)
        def _():
            zcopy(r).wait_recv()
            if r == 1:
                for d in (1, 3, 2):
                    xcopy(4, d).start()
        for k in SHARDS:
            @pl.when(yneed(k) & (yrow(k) == r) & shards(k))
            def _():
                ycopy(k, my_rows).start()
    for d in range(1, 4):
        xcopy(0, d).wait_recv()
    scopy(0).start()
    for k in DIRECT:
        @pl.when(first & (dp + 2 * k <= 31))
        def _():
            bcopy(k).start()
    for d in (1, 3, 2):
        wz1(d).start()
        wy1(d).start()

    def issue(k):
        @pl.when(shards(k) & has_src(k))
        def _():
            ycopy(k, my_rows).wait_recv()
            for d in (1, 3, 2):
                xcopy(k, d).start()

    def along(k):
        @pl.when(first & yneed(k))
        def _():
            ycopy(k, half).start()

    def weights2():
        wown.wait()
        for d in range(1, 4):
            wy1(d).wait_recv()
        for d in (1, 3, 2):
            wz2(d).start()
        for d in range(1, 4):
            wz1(d).wait_recv()
        for d in (1, 3, 2):
            wy2(d).start()

    def weights4():
        for d in range(1, 4):
            wz2(d).wait_recv()
        wsib(0).start()

    def weights5():
        for d in range(1, 4):
            wy2(d).wait_recv()
        wsib(1).start()

    def relay(k):
        if k in DIRECT + ALONG:
            @pl.when(first & has_src(k))
            def _():
                (bcopy(k) if k in DIRECT else ycopy(k, half)).wait_recv()
                scopy(k).start()

        @pl.when(has_src(k) & shards(k))
        def _():
            for d in range(1, 4):
                xcopy(k, d).wait_recv()
            scopy(k).start()

    def arrive(k):
        if k == 0:
            scopy(0).wait_recv()
        else:
            @pl.when(has_src(k))
            def _():
                scopy(k).wait_recv()

    def score(k, slot, first):
        for r in range(ROWS // R1):
            rows = pl.ds(r * R1, R1)
            s = lax.dot_general(qs[rows, :], kbuf[k], NT, preferred_element_type=F32)
            if k == 0:
                rr = lax.broadcasted_iota(jnp.int32, (R1, CHUNK), 0)
                cc = lax.broadcasted_iota(jnp.int32, (R1, CHUNK), 1)
                s = jnp.where(cc <= (rr & (TOK - 1)) + core * TOK, s, BIG)
            S[slot, rows, :] = s
            m = jnp.maximum(s[:, :128], s[:, 128:])
            mx[rows, :] = m if first else jnp.maximum(mx[rows, :], m)

    ps, ls = (p0, p1), (l0, l1)

    def weigh(gi, r):
        rows = pl.ds(r * R2, R2)
        m = jnp.max(mx[rows, :], axis=1, keepdims=True) * C
        n = len(GROUPS[gi])
        l = None
        for j in range(n):
            p = jnp.exp2(S[j, rows, :] * C - m)
            t = p[:, :128] + p[:, 128:]
            l = t if l is None else l + t
            ps[r % 2][:, j * CHUNK:(j + 1) * CHUNK] = p.astype(BF16)
        ls[r % 2][...] = l
        return m

    def gather_values(gi):
        ks = GROUPS[gi]
        return jnp.concatenate([kbuf[k, :, 0:LATENT] for k in ks], axis=0)

    def values(gi, r, m):
        rows = pl.ds(r * R2, R2)
        n = len(GROUPS[gi])
        a = jnp.dot(ps[r % 2][:, 0:n * CHUNK], gather_values(gi), preferred_element_type=F32)
        l = ls[r % 2][...]
        last = gi == len(GROUPS) - 1
        if gi > 0:
            al = jnp.exp2(mold[rows, 0:1] - m)
            a = a + acc[rows, :] * al
            l = l + lsum[rows, :] * al
        if last:
            inv = 1.0 / jnp.sum(l, axis=1, keepdims=True)
            ctx[rows, :] = (a * inv).astype(BF16)
        else:
            acc[rows, :] = a
            lsum[rows, :] = l
            mold[rows, :] = jnp.broadcast_to(m, (R2, 128))

    def finish(gi, between=()):
        n = ROWS // R2
        m = weigh(gi, 0)
        for r in range(n):
            nm = weigh(gi, r + 1) if r + 1 < n else None
            values(gi, r, m)
            m = nm
            if r < len(between) and between[r] is not None:
                between[r]()

    def ring8():
        @pl.when(z >= 2)
        def _():
            for d in (1, 3, 2):
                xcopy(8, d).start()

    arrive(0)
    score(0, 0, True)
    issue(1)
    issue(3)
    ring8()
    relay(4)
    issue(2)
    arrive(4)
    score(4, 1, False)
    relay(1)
    issue(6)
    issue(5)
    issue(7)
    weights2()
    arrive(1)
    score(1, 2, False)
    relay(3)
    relay(8)
    along(5)
    along(7)
    arrive(3)
    score(3, 3, False)
    finish(0, [None, lambda: relay(2)])
    arrive(8)
    score(8, 0, False)
    relay(6)
    arrive(2)
    score(2, 1, False)
    relay(5)
    arrive(6)
    score(6, 2, False)
    relay(7)
    arrive(5)
    score(5, 3, False)
    arrive(7)
    score(7, 4, False)
    weights4()
    finish(1, [None, weights5])

    for h in range(HEADS):
        if h % H2 == 0:
            wsib(h // H2).wait_recv()
        wv = wbuf[h].reshape(LATENT, VALUE)
        o_ref[:, h * VALUE:(h + 1) * VALUE] = jnp.dot(ctx[h * TOK:(h + 1) * TOK, :], wv, preferred_element_type=F32).astype(BF16)

    for d in range(1, 4):
        xcopy(0, d).wait_send()
        wy1(d).wait_send()
        wz1(d).wait_send()
        wy2(d).wait_send()
        wz2(d).wait_send()
    wsib(0).wait_send()
    wsib(1).wait_send()
    for r in (1, 2):
        @pl.when(z + r <= 3)
        def _():
            zcopy(r).wait_send()

    for k in SHARDS:
        @pl.when(yneed(k) & shards(k))
        def _():
            ycopy(k, my_rows).wait_send()
    for k in DIRECT:
        @pl.when(first & (dp + 2 * k <= 31))
        def _():
            bcopy(k).wait_send()
    for k in ALONG:
        @pl.when(first & yneed(k))
        def _():
            ycopy(k, half).wait_send()

    scopy(0).wait_send()
    for k in range(1, NCH):
        @pl.when(has_src(k))
        def _():
            scopy(k).wait_send()

        @pl.when(has_src(k) & shards(k))
        def _():
            for d in range(1, 4):
                xcopy(k, d).wait_send()


def per_device(queries, latents, segment_ids, value_weight):
    dma = pltpu.SemaphoreType.DMA
    gmax = max(len(g) for g in GROUPS)
    return pl.pallas_call(
        kernel,
        out_shape=jax.ShapeDtypeStruct((TOK, HEADS * VALUE), BF16),
        in_specs=[pl.BlockSpec(memory_space=pl.ANY), pl.BlockSpec(memory_space=pltpu.VMEM), pl.BlockSpec(memory_space=pltpu.VMEM), pl.BlockSpec(memory_space=pl.ANY)],
        out_specs=pl.BlockSpec(memory_space=pltpu.VMEM),
        scratch_shapes=[
            pltpu.VMEM((NCH, CHUNK, WIDE), BF16),
            pltpu.VMEM((HEADS, 4, 4, 2, 16, VALUE), BF16),
            pltpu.VMEM((HEADS // 2, TOK, 2 * FEAT), BF16),
            pltpu.VMEM((ROWS, WIDE), BF16),
            pltpu.VMEM((TOK, 128), F32),
            pltpu.VMEM((gmax, ROWS, CHUNK), F32),
            pltpu.VMEM((ROWS, 128), F32),
            pltpu.VMEM((R2, gmax * CHUNK), BF16),
            pltpu.VMEM((R2, gmax * CHUNK), BF16),
            pltpu.VMEM((R2, 128), F32),
            pltpu.VMEM((R2, 128), F32),
            pltpu.VMEM((ROWS, 128), F32),
            pltpu.VMEM((ROWS, 128), F32),
            pltpu.VMEM((ROWS, LATENT), F32),
            pltpu.VMEM((ROWS, LATENT), BF16),
            dma((HEADS // 2,)), dma((1,)),
            dma((NCH, 4)), dma((NCH, 4)),
            dma((NCH,)), dma((NCH,)), dma((NCH,)),
            dma((3,)), dma((3,)),
            dma((NCH,)), dma((NCH,)),
            dma((2, 4)), dma((2, 4)),
            dma((2, 4)), dma((2, 4)),
            dma((2,)), dma((2,)),
        ],
        compiler_params=pltpu.CompilerParams(collective_id=0, has_side_effects=True, vmem_limit_bytes=56 * 2 ** 20),
        cost_estimate=pl.CostEstimate(flops=11 * 10 ** 9, bytes_accessed=8 * 10 ** 6, transcendentals=5 * 10 ** 6),
    )(queries, latents, segment_ids.reshape(1, TOK), value_weight)


def solution(mesh):
    placed = (P("dp", "tp"), P(("dp", "tp"), None), P("dp"), P("tp", "dp", None))
    return jax.shard_map(per_device, mesh=mesh, in_specs=placed, out_specs=P("dp", "tp"), check_vma=False)
```

```python
import functools

import jax
import jax.numpy as jnp
from jax import lax
from jax.experimental import pallas as pl
from jax.experimental.pallas import tpu as pltpu
from jax.sharding import PartitionSpec as P

MESH = pl.DeviceIdType.MESH
F32, BF16 = jnp.float32, jnp.bfloat16
LATENT, ROPE, VALUE = 512, 64, 128
FEAT = LATENT + ROPE
WIDE = 640
TOK = 128
HEADS = 16
ROWS = TOK * HEADS
CHUNK = 2 * TOK
NCH = 9
SHARD = 32
DIRECT = (1, 3)
ALONG = (5, 7)
SHARDS = (1, 3, 2, 6, 5, 7)
RB = 512
STEPS = ((0,), (4, 8), (1, 3), (2, 6), (5, 7))
C = 192.0 ** -0.5 * 1.4426950408889634
BIG = -1.0e30
NT = (((1,), (1,)), ((), ()))


def kernel(q_hbm, lat_hbm, seg_hbm, w_hbm, o_ref,
           lat_ref, seg_ref, in_sem, kbuf, wbuf, qv, qs, segc, S, mx, lsum, top, acc, ctx,
           q_sem, w_sem, sx, rx, sb, sy, ry, sz, rz, ss, rs, swy, rwy, swz, rwz, sws, rws):
    dp, tp = lax.axis_index("dp"), lax.axis_index("tp")
    core = lax.rem(dp, 2)
    y = lax.rem(dp // 2, 4)
    z = dp // 8
    sib = dp + 1 - 2 * core

    def xpeer(d):
        return (dp, lax.rem(tp + d, 4))

    def ypeer(d):
        return (z * 8 + lax.rem(y + d, 4) * 2 + core, tp)

    def zpeer(d):
        return (lax.rem(z + d, 4) * 8 + y * 2 + core, tp)

    def has_src(k):
        return dp - 2 * k >= 0

    icopy = [pltpu.make_async_copy(lat_hbm, lat_ref, in_sem.at[0]), pltpu.make_async_copy(seg_hbm, seg_ref, in_sem.at[1])]
    for cp in icopy:
        cp.start()
    qcopy = [pltpu.make_async_copy(q_hbm.at[:, pl.ds(g * 2 * FEAT, 2 * FEAT)], qv.at[g], q_sem.at[g]) for g in range(HEADS // 2)]
    for cp in qcopy:
        cp.start()
    wown = pltpu.make_async_copy(w_hbm, wbuf.at[:, z, y, core], w_sem.at[0])
    wown.start()

    barrier = pltpu.get_barrier_semaphore()

    def greet(dev):
        pl.semaphore_signal(barrier, inc=1, device_id=dev, device_id_type=MESH)

    for d in range(1, 4):
        greet(xpeer(d))
        greet(ypeer(d))
        greet(zpeer(d))
    greet((sib, tp))
    for k in DIRECT:
        @pl.when((core == 0) & has_src(k))
        def _():
            greet((dp - 2 * k, tp))

    for cp in icopy:
        cp.wait()
    seg = jnp.broadcast_to(seg_ref[...].astype(F32), (TOK, TOK))
    segc[...] = jnp.transpose(seg)
    my_rows = pl.ds(pl.multiple_of(core * TOK + tp * SHARD, SHARD), SHARD)
    half = pl.ds(pl.multiple_of(core * TOK, TOK), TOK)
    other = pl.ds(pl.multiple_of((1 - core) * TOK, TOK), TOK)
    lane32 = lax.broadcasted_iota(jnp.int32, (SHARD, 128), 1).astype(F32)
    mine = segc[pl.ds(pl.multiple_of(tp * SHARD, SHARD), SHARD), :]
    kfeat = jnp.where((lane32 >= 4.0) | (lane32 == mine), 0.0, BIG).astype(BF16)
    kbuf[0, my_rows, 0:FEAT] = lat_ref[...]
    kbuf[0, my_rows, FEAT:WIDE] = kfeat[:, :WIDE - FEAT]

    n_wait = 10 + jnp.where(core == 0, jnp.where(dp + 2 <= 31, 1, 0) + jnp.where(dp + 6 <= 31, 1, 0), 0)
    pl.semaphore_wait(barrier, n_wait)

    def remote(ref, dst, ssem, rsem, dev):
        return pltpu.make_async_remote_copy(ref, dst, ssem, rsem, device_id=dev, device_id_type=MESH)

    def zdev(v):
        return (v * 8 + y * 2 + core, tp)

    def xcopy(k, d):
        at = kbuf.at[k, my_rows, :]
        return remote(at, at, sx.at[k], rx.at[k], xpeer(d))

    def xthree(k):
        at = kbuf.at[k, pl.ds(0, 3 * SHARD), :]
        return remote(at, at, sx.at[k], rx.at[k], xpeer(1))

    def zcopy(r):
        return remote(kbuf.at[0, my_rows, :], kbuf.at[4 * r, my_rows, :], sz.at[r], rz.at[r], zdev(lax.rem(z + r, 4)))

    first = core == 0
    second = core == 1

    def yrow(k):
        return k // 4 + jnp.where(y + k % 4 <= 3, 0, 1)

    def ycopy(k, rows):
        return remote(kbuf.at[4 * yrow(k), rows, :], kbuf.at[k, rows, :], sy.at[k], ry.at[k], ypeer(k % 4))

    def yneed(k):
        return z >= yrow(k)

    def bcopy(k):
        return remote(kbuf.at[0, half, :], kbuf.at[k, half, :], sb.at[k], ry.at[k], (dp + 2 * k, tp))

    def scopy(k):
        at = kbuf.at[k, half, :]
        return remote(at, at, ss.at[k], rs.at[k], (sib, tp))

    H2 = HEADS // 2

    lo, hi = pl.ds(0, H2), pl.ds(H2, H2)

    def wy1(d):
        return remote(w_hbm.at[lo], wbuf.at[lo, z, y, core], swy.at[0], rwy.at[0], ypeer(d))

    def wz1(d):
        return remote(w_hbm.at[hi], wbuf.at[hi, z, y, core], swz.at[0], rwz.at[0], zpeer(d))

    def wz2(d):
        at = wbuf.at[lo, z, :, core]
        return remote(at, at, swz.at[1], rwz.at[1], zpeer(d))

    def wy2(d):
        at = wbuf.at[hi, :, y, core]
        return remote(at, at, swy.at[1], rwy.at[1], ypeer(d))

    def wthree(along_y, stage):
        at = wbuf.at[lo, pl.ds(0, 3), 0, 0] if stage == 0 else wbuf.at[lo, pl.ds(0, 3), :, 0]
        if along_y:
            return remote(at, at, swy.at[stage], rwy.at[stage], ypeer(1))
        return remote(at, at, swz.at[stage], rwz.at[stage], zpeer(1))

    def wsib(i):
        at = wbuf.at[(lo, hi)[i], :, :, core]
        return remote(at, at, sws.at[i], rws.at[i], (sib, tp))

    def shards(k):
        return second if k in DIRECT + ALONG else True

    for r in (1, 2):
        @pl.when(z + r <= 3)
        def _():
            zcopy(r).start()
    for d in (1, 3, 2):
        xcopy(0, d).start()
    for k in SHARDS:
        @pl.when((yrow(k) == 0) & shards(k))
        def _():
            ycopy(k, my_rows).start()

    segv = segc[...]
    lane = lax.broadcasted_iota(jnp.int32, (TOK, 128), 1)
    onehot = jnp.where((lane - 64).astype(F32) == segv, 1.0, 0.0)

    def prep(g):
        qcopy[g].wait()
        even = qv[g, :, 0:WIDE]
        odd = pltpu.roll(qv[g, :, LATENT:2 * FEAT], WIDE - 64, 1)
        for i, v in ((0, even), (1, odd)):
            r = pl.ds((2 * g + i) * TOK, TOK)
            qs[r, 0:LATENT] = v[:, 0:LATENT]
            qs[r, LATENT:WIDE] = jnp.where(lane < 64, v[:, LATENT:WIDE].astype(F32), onehot).astype(BF16)

    for k in range(1, NCH):
        @pl.when(jnp.logical_not(has_src(k)))
        def _():
            ln = lax.broadcasted_iota(jnp.int32, (CHUNK, 128), 1)
            kbuf[k, :, 0:LATENT] = jnp.zeros((CHUNK, LATENT), BF16)
            kbuf[k, :, LATENT:WIDE] = jnp.where((ln >= 64) & (ln < 68), BIG, 0.0).astype(BF16)

    for g in range(HEADS // 2):
        prep(g)

    for r in (1, 2):
        @pl.when(z >= r)
        def _():
            zcopy(r).wait_recv()
            for d in (1, 3, 2):
                xcopy(4 * r, d).start()
        for k in SHARDS:
            @pl.when(yneed(k) & (yrow(k) == r) & shards(k))
            def _():
                ycopy(k, my_rows).start()
    for d in (1, 3, 2):
        wz1(d).start()
        wy1(d).start()
    xthree(0).wait_recv()
    scopy(0).start()
    for k in DIRECT:
        @pl.when(first & (dp + 2 * k <= 31))
        def _():
            bcopy(k).start()
    def issue(k):
        @pl.when(shards(k) & has_src(k))
        def _():
            ycopy(k, my_rows).wait_recv()
            for d in (1, 3, 2):
                xcopy(k, d).start()

    def along(k, r):
        @pl.when(first & yneed(k) & (yrow(k) == r))
        def _():
            ycopy(k, half).start()

    def weights2():
        wown.wait()
        wthree(True, 0).wait_recv()
        for d in (1, 3, 2):
            wz2(d).start()
        wthree(False, 0).wait_recv()
        for d in (1, 3, 2):
            wy2(d).start()

    def weights4():
        wthree(False, 1).wait_recv()
        wsib(0).start()

    def weights5():
        wthree(True, 1).wait_recv()
        wsib(1).start()

    def relay(k, who=None):
        if k in DIRECT + ALONG:
            @pl.when(first & has_src(k))
            def _():
                (bcopy(k) if k in DIRECT else ycopy(k, half)).wait_recv()
                scopy(k).start()

        mine = shards(k) if who is None else who

        @pl.when(has_src(k) & mine)
        def _():
            xthree(k).wait_recv()
            scopy(k).start()

    def arrive(k):
        if k == 0:
            scopy(0).wait_recv()
        else:
            @pl.when(has_src(k))
            def _():
                scopy(k).wait_recv()

    def score(ks, slot, r):
        rows = pl.ds(r * RB, RB)
        best = None
        for j, k in enumerate(ks):
            s = lax.dot_general(qs[rows, :], kbuf[k], NT, preferred_element_type=F32)
            if k == 0:
                rr = lax.broadcasted_iota(jnp.int32, (RB, CHUNK), 0)
                cc = lax.broadcasted_iota(jnp.int32, (RB, CHUNK), 1)
                s = jnp.where(cc <= (rr & (TOK - 1)) + core * TOK, s, BIG)
            S[slot, j, rows, :] = s
            m = jnp.maximum(s[:, :128], s[:, 128:])
            best = m if best is None else jnp.maximum(best, m)
        mx[slot, rows, :] = best

    def values(ks, slot, r, begin, last):
        rows = pl.ds(r * RB, RB)
        m = jnp.max(mx[slot, rows, :], axis=1, keepdims=True) * C
        if not begin:
            m = jnp.maximum(m, top[rows, 0:1])
        l, ps = None, []
        for j in range(len(ks)):
            p = jnp.exp2(S[slot, j, rows, :] * C - m)
            t = p[:, :128] + p[:, 128:]
            l = t if l is None else l + t
            ps.append(p.astype(BF16))
        p = jnp.concatenate(ps, axis=1) if len(ks) > 1 else ps[0]
        v = jnp.concatenate([kbuf[k, :, 0:LATENT] for k in ks], axis=0)
        a = jnp.dot(p, v, preferred_element_type=F32)
        if not begin:
            al = jnp.exp2(top[rows, 0:1] - m)
            a = a + acc[rows, :] * al
            l = l + lsum[rows, :] * al
        if last:
            inv = 1.0 / jnp.sum(l, axis=1, keepdims=True)
            ctx[rows, :] = (a * inv).astype(BF16)
        else:
            acc[rows, :] = a
            lsum[rows, :] = l
            top[rows, :] = jnp.broadcast_to(m, (RB, 128))

    def step(i):
        for r in range(ROWS // RB):
            if i < len(STEPS):
                score(STEPS[i], i % 2, r)
            if i > 0:
                values(STEPS[i - 1], (i - 1) % 2, r, i == 1, i == len(STEPS))

    issue(1)
    issue(3)
    arrive(0)
    step(0)
    issue(2)
    issue(6)
    issue(5)
    issue(7)
    relay(4)
    along(5, 1)
    along(7, 1)
    relay(8)
    along(5, 2)
    along(7, 2)
    weights2()
    arrive(4)
    arrive(8)
    step(1)
    relay(1)
    relay(3)
    arrive(1)
    arrive(3)
    step(2)
    relay(2)
    relay(6)
    relay(5)
    relay(7)
    arrive(2)
    arrive(6)
    step(3)
    arrive(5)
    arrive(7)
    weights4()
    step(4)
    weights5()
    step(5)

    for h in range(HEADS):
        if h % H2 == 0:
            wsib(h // H2).wait_recv()
        wv = wbuf[h].reshape(LATENT, VALUE)
        o_ref[:, h * VALUE:(h + 1) * VALUE] = jnp.dot(ctx[h * TOK:(h + 1) * TOK, :], wv, preferred_element_type=F32).astype(BF16)

    xthree(0).wait_send()
    for stage in range(2):
        wthree(True, stage).wait_send()
        wthree(False, stage).wait_send()
        wsib(stage).wait_send()
    for r in (1, 2):
        @pl.when(z + r <= 3)
        def _():
            zcopy(r).wait_send()

    for k in SHARDS:
        @pl.when(yneed(k) & shards(k))
        def _():
            ycopy(k, my_rows).wait_send()
    for k in DIRECT:
        @pl.when(first & (dp + 2 * k <= 31))
        def _():
            bcopy(k).wait_send()
    for k in ALONG:
        @pl.when(first & yneed(k))
        def _():
            ycopy(k, half).wait_send()

    scopy(0).wait_send()
    for k in range(1, NCH):
        @pl.when(has_src(k))
        def _():
            scopy(k).wait_send()

        @pl.when(has_src(k) & shards(k))
        def _():
            xthree(k).wait_send()


def per_device(queries, latents, segment_ids, value_weight):
    dma = pltpu.SemaphoreType.DMA
    return pl.pallas_call(
        kernel,
        out_shape=pltpu.VMEM((TOK, HEADS * VALUE), BF16),
        in_specs=[pl.BlockSpec(memory_space=pltpu.HBM)] * 4,
        out_specs=pl.BlockSpec(memory_space=pltpu.VMEM),
        scratch_shapes=[
            pltpu.VMEM((SHARD, FEAT), BF16), pltpu.VMEM((1, TOK), jnp.int32), dma((2,)),
            pltpu.VMEM((NCH, CHUNK, WIDE), BF16),
            pltpu.VMEM((HEADS, 4, 4, 2, 16, VALUE), BF16),
            pltpu.VMEM((HEADS // 2, TOK, 2 * FEAT), BF16),
            pltpu.VMEM((ROWS, WIDE), BF16),
            pltpu.VMEM((TOK, 128), F32),
            pltpu.VMEM((2, max(len(g) for g in STEPS), ROWS, CHUNK), F32),
            pltpu.VMEM((2, ROWS, 128), F32),
            pltpu.VMEM((ROWS, 128), F32),
            pltpu.VMEM((ROWS, 128), F32),
            pltpu.VMEM((ROWS, LATENT), F32),
            pltpu.VMEM((ROWS, LATENT), BF16),
            dma((HEADS // 2,)), dma((1,)),
            dma((NCH,)), dma((NCH,)),
            dma((NCH,)), dma((NCH,)), dma((NCH,)),
            dma((3,)), dma((3,)),
            dma((NCH,)), dma((NCH,)),
            dma((2,)), dma((2,)),
            dma((2,)), dma((2,)),
            dma((2,)), dma((2,)),
        ],
        compiler_params=pltpu.CompilerParams(collective_id=0, has_side_effects=True, vmem_limit_bytes=48 * 2 ** 20),
        cost_estimate=pl.CostEstimate(flops=11 * 10 ** 9, bytes_accessed=8 * 10 ** 6, transcendentals=5 * 10 ** 6),
    )(*[pltpu.with_memory_space_constraint(x, pltpu.HBM) for x in (queries, latents, segment_ids.reshape(1, TOK), value_weight)])


def solution(mesh):
    placed = (P("dp", "tp"), P(("dp", "tp"), None), P("dp"), P("tp", "dp", None))
    return jax.shard_map(per_device, mesh=mesh, in_specs=placed, out_specs=P("dp", "tp"), check_vma=False)
```

```python
import functools

import jax
import jax.numpy as jnp
from jax import lax
from jax.experimental import pallas as pl
from jax.experimental.pallas import tpu as pltpu
from jax.sharding import PartitionSpec as P

MESH = pl.DeviceIdType.MESH
F32, BF16 = jnp.float32, jnp.bfloat16
LATENT, ROPE, VALUE = 512, 64, 128
FEAT = LATENT + ROPE
WIDE = 640
TOK = 128
HEADS = 16
ROWS = TOK * HEADS
CHUNK = 2 * TOK
NCH = 9
SHARD = 32
DIRECT = (1, 3)
ALONG = (5, 7)
SHARDS = (1, 3, 2, 6, 5, 7)
YFIRST = 6
RB = 1024
STEPS = ((0,), (4,), (8, 1), (3, 2), (6, 5, 7))
C = 192.0 ** -0.5 * 1.4426950408889634
BIG = -1.0e30
NT = (((1,), (1,)), ((), ()))


def kernel(q_hbm, lat_hbm, seg_hbm, w_hbm, o_ref,
           lat_ref, seg_ref, in_sem, kbuf, wbuf, qv, qs, segc, S, mx, lsum, top, acc, ctx,
           q_sem, w_sem, sx, rx, sb, sy, ry, sz, rz, ss, rs, swy, rwy, swz, rwz, sws, rws):
    dp, tp = lax.axis_index("dp"), lax.axis_index("tp")
    core = lax.rem(dp, 2)
    y = lax.rem(dp // 2, 4)
    z = dp // 8
    sib = dp + 1 - 2 * core

    def xpeer(d):
        return (dp, lax.rem(tp + d, 4))

    def ypeer(d):
        return (z * 8 + lax.rem(y + d, 4) * 2 + core, tp)

    def zpeer(d):
        return (lax.rem(z + d, 4) * 8 + y * 2 + core, tp)

    def has_src(k):
        return dp - 2 * k >= 0

    icopy = [pltpu.make_async_copy(lat_hbm, lat_ref, in_sem.at[0]), pltpu.make_async_copy(seg_hbm, seg_ref, in_sem.at[1])]
    for cp in icopy:
        cp.start()
    qcopy = [pltpu.make_async_copy(q_hbm.at[:, pl.ds(g * 2 * FEAT, 2 * FEAT)], qv.at[g], q_sem.at[g]) for g in range(HEADS // 2)]
    for cp in qcopy:
        cp.start()
    wown = pltpu.make_async_copy(w_hbm, wbuf.at[:, z, y, core], w_sem.at[0])
    wown.start()

    barrier = pltpu.get_barrier_semaphore()

    def greet(dev):
        pl.semaphore_signal(barrier, inc=1, device_id=dev, device_id_type=MESH)

    for d in range(1, 4):
        greet(xpeer(d))
        greet(ypeer(d))
        greet(zpeer(d))
    greet((sib, tp))
    for k in DIRECT:
        @pl.when((core == 0) & has_src(k))
        def _():
            greet((dp - 2 * k, tp))

    for cp in icopy:
        cp.wait()
    seg = jnp.broadcast_to(seg_ref[...].astype(F32), (TOK, TOK))
    segc[...] = jnp.transpose(seg)
    my_rows = pl.ds(pl.multiple_of(core * TOK + tp * SHARD, SHARD), SHARD)
    half = pl.ds(pl.multiple_of(core * TOK, TOK), TOK)
    other = pl.ds(pl.multiple_of((1 - core) * TOK, TOK), TOK)
    lane32 = lax.broadcasted_iota(jnp.int32, (SHARD, 128), 1).astype(F32)
    mine = segc[pl.ds(pl.multiple_of(tp * SHARD, SHARD), SHARD), :]
    kfeat = jnp.where((lane32 >= 4.0) | (lane32 == mine), 0.0, BIG).astype(BF16)
    kbuf[0, my_rows, 0:FEAT] = lat_ref[...]
    kbuf[0, my_rows, FEAT:WIDE] = kfeat[:, :WIDE - FEAT]

    n_wait = 10 + jnp.where(core == 0, jnp.where(dp + 2 <= 31, 1, 0) + jnp.where(dp + 6 <= 31, 1, 0), 0)
    pl.semaphore_wait(barrier, n_wait)

    def remote(ref, dst, ssem, rsem, dev):
        return pltpu.make_async_remote_copy(ref, dst, ssem, rsem, device_id=dev, device_id_type=MESH)

    def zdev(v):
        return (v * 8 + y * 2 + core, tp)

    def xcopy(k, d):
        at = kbuf.at[k, my_rows, :]
        return remote(at, at, sx.at[k], rx.at[k], xpeer(d))

    def xthree(k):
        at = kbuf.at[k, pl.ds(0, 3 * SHARD), :]
        return remote(at, at, sx.at[k], rx.at[k], xpeer(1))

    def zcopy(r):
        return remote(kbuf.at[0, my_rows, :], kbuf.at[4 * r, my_rows, :], sz.at[r], rz.at[r], zdev(lax.rem(z + r, 4)))

    first = core == 0
    second = core == 1

    def yrow(k):
        return k // 4 + jnp.where(y + k % 4 <= 3, 0, 1)

    def ycopy(k, rows):
        return remote(kbuf.at[4 * yrow(k), rows, :], kbuf.at[k, rows, :], sy.at[k], ry.at[k], ypeer(k % 4))

    def yneed(k):
        return z >= yrow(k)

    def bcopy(k):
        return remote(kbuf.at[0, half, :], kbuf.at[k, half, :], sb.at[k], ry.at[k], (dp + 2 * k, tp))

    def scopy(k):
        at = kbuf.at[k, half, :]
        return remote(at, at, ss.at[k], rs.at[k], (sib, tp))


    lo, hi = pl.ds(0, YFIRST), pl.ds(YFIRST, HEADS - YFIRST)

    def wy1(d):
        return remote(w_hbm.at[lo], wbuf.at[lo, z, y, core], swy.at[0], rwy.at[0], ypeer(d))

    def wz1(d):
        return remote(w_hbm.at[hi], wbuf.at[hi, z, y, core], swz.at[0], rwz.at[0], zpeer(d))

    def wz2(d):
        at = wbuf.at[lo, z, :, core]
        return remote(at, at, swz.at[1], rwz.at[1], zpeer(d))

    def wy2(d):
        at = wbuf.at[hi, :, y, core]
        return remote(at, at, swy.at[1], rwy.at[1], ypeer(d))

    def wthree(along_y, stage):
        heads = lo if along_y == (stage == 0) else hi
        at = wbuf.at[heads, pl.ds(0, 3), 0, 0] if stage == 0 else wbuf.at[heads, pl.ds(0, 3), :, 0]
        if along_y:
            return remote(at, at, swy.at[stage], rwy.at[stage], ypeer(1))
        return remote(at, at, swz.at[stage], rwz.at[stage], zpeer(1))

    def wsib(i):
        at = wbuf.at[(lo, hi)[i], :, :, core]
        return remote(at, at, sws.at[i], rws.at[i], (sib, tp))

    def shards(k):
        return second if k in DIRECT + ALONG else True

    for r in (1, 2):
        @pl.when(z + r <= 3)
        def _():
            zcopy(r).start()
    for d in (1, 3, 2):
        xcopy(0, d).start()
    for k in SHARDS:
        @pl.when((yrow(k) == 0) & shards(k))
        def _():
            ycopy(k, my_rows).start()

    segv = segc[...]
    lane = lax.broadcasted_iota(jnp.int32, (TOK, 128), 1)
    onehot = jnp.where((lane - 64).astype(F32) == segv, 1.0, 0.0)

    def prep(g):
        qcopy[g].wait()
        even = qv[g, :, 0:WIDE]
        odd = pltpu.roll(qv[g, :, LATENT:2 * FEAT], WIDE - 64, 1)
        for i, v in ((0, even), (1, odd)):
            r = pl.ds((2 * g + i) * TOK, TOK)
            qs[r, 0:LATENT] = v[:, 0:LATENT]
            qs[r, LATENT:WIDE] = jnp.where(lane < 64, v[:, LATENT:WIDE].astype(F32), onehot).astype(BF16)

    for k in range(1, NCH):
        @pl.when(jnp.logical_not(has_src(k)))
        def _():
            ln = lax.broadcasted_iota(jnp.int32, (CHUNK, 128), 1)
            kbuf[k, :, 0:LATENT] = jnp.zeros((CHUNK, LATENT), BF16)
            kbuf[k, :, LATENT:WIDE] = jnp.where((ln >= 64) & (ln < 68), BIG, 0.0).astype(BF16)

    for g in range(HEADS // 2):
        prep(g)

    for r in (1, 2):
        @pl.when(z >= r)
        def _():
            zcopy(r).wait_recv()
            for d in (1, 3, 2):
                xcopy(4 * r, d).start()
        for k in SHARDS:
            @pl.when(yneed(k) & (yrow(k) == r) & shards(k))
            def _():
                ycopy(k, my_rows).start()
    for d in (1, 3, 2):
        wz1(d).start()
        wy1(d).start()
    xthree(0).wait_recv()
    scopy(0).start()
    for k in DIRECT:
        @pl.when(first & (dp + 2 * k <= 31))
        def _():
            bcopy(k).start()
    def issue(k):
        @pl.when(shards(k) & has_src(k))
        def _():
            ycopy(k, my_rows).wait_recv()
            for d in (1, 3, 2):
                xcopy(k, d).start()

    def along(k, r):
        @pl.when(first & yneed(k) & (yrow(k) == r))
        def _():
            ycopy(k, half).start()

    def weights2():
        wown.wait()
        wthree(True, 0).wait_recv()
        for d in (1, 3, 2):
            wz2(d).start()
        wthree(False, 0).wait_recv()
        for d in (1, 3, 2):
            wy2(d).start()

    def weights4():
        wthree(False, 1).wait_recv()
        wsib(0).start()

    def weights5():
        wthree(True, 1).wait_recv()
        wsib(1).start()

    def relay(k, who=None):
        if k in DIRECT + ALONG:
            @pl.when(first & has_src(k))
            def _():
                (bcopy(k) if k in DIRECT else ycopy(k, half)).wait_recv()
                scopy(k).start()

        mine = shards(k) if who is None else who

        @pl.when(has_src(k) & mine)
        def _():
            xthree(k).wait_recv()
            scopy(k).start()

    def arrive(k):
        if k == 0:
            scopy(0).wait_recv()
        else:
            @pl.when(has_src(k))
            def _():
                scopy(k).wait_recv()

    def score(ks, slot, r):
        rows = pl.ds(r * RB, RB)
        best = None
        for j, k in enumerate(ks):
            s = lax.dot_general(qs[rows, :], kbuf[k], NT, preferred_element_type=F32)
            if k == 0:
                rr = lax.broadcasted_iota(jnp.int32, (RB, CHUNK), 0)
                cc = lax.broadcasted_iota(jnp.int32, (RB, CHUNK), 1)
                s = jnp.where(cc <= (rr & (TOK - 1)) + core * TOK, s, BIG)
            S[slot, j, rows, :] = s
            m = jnp.maximum(s[:, :128], s[:, 128:])
            best = m if best is None else jnp.maximum(best, m)
        mx[slot, rows, :] = best

    def values(ks, slot, r, begin, last):
        rows = pl.ds(r * RB, RB)
        m = jnp.max(mx[slot, rows, :], axis=1, keepdims=True) * C
        if not begin:
            m = jnp.maximum(m, top[rows, 0:1])
        l, ps = None, []
        for j in range(len(ks)):
            p = jnp.exp2(S[slot, j, rows, :] * C - m)
            t = p[:, :128] + p[:, 128:]
            l = t if l is None else l + t
            ps.append(p.astype(BF16))
        p = jnp.concatenate(ps, axis=1) if len(ks) > 1 else ps[0]
        v = jnp.concatenate([kbuf[k, :, 0:LATENT] for k in ks], axis=0)
        a = jnp.dot(p, v, preferred_element_type=F32)
        if not begin:
            al = jnp.exp2(top[rows, 0:1] - m)
            a = a + acc[rows, :] * al
            l = l + lsum[rows, :] * al
        if last:
            inv = 1.0 / jnp.sum(l, axis=1, keepdims=True)
            ctx[rows, :] = (a * inv).astype(BF16)
        else:
            acc[rows, :] = a
            lsum[rows, :] = l
            top[rows, :] = jnp.broadcast_to(m, (RB, 128))

    def step(i):
        for r in range(ROWS // RB):
            if i < len(STEPS):
                score(STEPS[i], i % 2, r)
            if i > 0:
                values(STEPS[i - 1], (i - 1) % 2, r, i == 1, i == len(STEPS))

    def early():
        xthree(0).wait_send()
        scopy(0).wait_send()
        wthree(True, 0).wait_send()
        wthree(False, 0).wait_send()
        for r in (1, 2):
            @pl.when(z + r <= 3)
            def _():
                zcopy(r).wait_send()

            @pl.when(z >= r)
            def _():
                xthree(4 * r).wait_send()
                scopy(4 * r).wait_send()
        for k in SHARDS:
            @pl.when(yneed(k) & shards(k))
            def _():
                ycopy(k, my_rows).wait_send()
        for k in DIRECT:
            @pl.when(first & (dp + 2 * k <= 31))
            def _():
                bcopy(k).wait_send()

    issue(1)
    arrive(0)
    step(0)
    issue(3)
    issue(2)
    issue(6)
    issue(5)
    issue(7)
    relay(4)
    along(5, 1)
    along(7, 1)
    relay(8)
    along(5, 2)
    along(7, 2)
    weights2()
    arrive(4)
    step(1)
    relay(1)
    relay(3)
    arrive(8)
    arrive(1)
    step(2)
    relay(2)
    relay(6)
    early()
    relay(5)
    relay(7)
    arrive(3)
    arrive(2)
    step(3)
    weights4()
    weights5()
    arrive(6)
    arrive(5)
    arrive(7)
    step(4)
    wsib(0).wait_recv()
    wsib(1).wait_recv()
    step(len(STEPS))
    for h in range(HEADS):
        wv = wbuf[h].reshape(LATENT, VALUE)
        o_ref[:, h * VALUE:(h + 1) * VALUE] = jnp.dot(ctx[h * TOK:(h + 1) * TOK, :], wv, preferred_element_type=F32).astype(BF16)
    wthree(True, 1).wait_send()
    wthree(False, 1).wait_send()
    wsib(0).wait_send()
    wsib(1).wait_send()
    for k in ALONG:
        @pl.when(first & yneed(k))
        def _():
            ycopy(k, half).wait_send()
    for k in SHARDS:
        @pl.when(has_src(k))
        def _():
            scopy(k).wait_send()

        @pl.when(has_src(k) & shards(k))
        def _():
            xthree(k).wait_send()


def per_device(queries, latents, segment_ids, value_weight):
    dma = pltpu.SemaphoreType.DMA
    return pl.pallas_call(
        kernel,
        out_shape=pltpu.VMEM((TOK, HEADS * VALUE), BF16),
        in_specs=[pl.BlockSpec(memory_space=pltpu.HBM)] * 4,
        out_specs=pl.BlockSpec(memory_space=pltpu.VMEM),
        scratch_shapes=[
            pltpu.VMEM((SHARD, FEAT), BF16), pltpu.VMEM((1, TOK), jnp.int32), dma((2,)),
            pltpu.VMEM((NCH, CHUNK, WIDE), BF16),
            pltpu.VMEM((HEADS, 4, 4, 2, 16, VALUE), BF16),
            pltpu.VMEM((HEADS // 2, TOK, 2 * FEAT), BF16),
            pltpu.VMEM((ROWS, WIDE), BF16),
            pltpu.VMEM((TOK, 128), F32),
            pltpu.VMEM((2, max(len(g) for g in STEPS), ROWS, CHUNK), F32),
            pltpu.VMEM((2, ROWS, 128), F32),
            pltpu.VMEM((ROWS, 128), F32),
            pltpu.VMEM((ROWS, 128), F32),
            pltpu.VMEM((ROWS, LATENT), F32),
            pltpu.VMEM((ROWS, LATENT), BF16),
            dma((HEADS // 2,)), dma((1,)),
            dma((NCH,)), dma((NCH,)),
            dma((NCH,)), dma((NCH,)), dma((NCH,)),
            dma((3,)), dma((3,)),
            dma((NCH,)), dma((NCH,)),
            dma((2,)), dma((2,)),
            dma((2,)), dma((2,)),
            dma((2,)), dma((2,)),
        ],
        compiler_params=pltpu.CompilerParams(collective_id=0, has_side_effects=True, vmem_limit_bytes=48 * 2 ** 20),
        cost_estimate=pl.CostEstimate(flops=11 * 10 ** 9, bytes_accessed=8 * 10 ** 6, transcendentals=5 * 10 ** 6),
    )(*[pltpu.with_memory_space_constraint(x, pltpu.HBM) for x in (queries, latents, segment_ids.reshape(1, TOK), value_weight)])


def solution(mesh):
    placed = (P("dp", "tp"), P(("dp", "tp"), None), P("dp"), P("tp", "dp", None))
    return jax.shard_map(per_device, mesh=mesh, in_specs=placed, out_specs=P("dp", "tp"), check_vma=False)
```

```python
import functools

import jax
import jax.numpy as jnp
from jax import lax
from jax.experimental import pallas as pl
from jax.experimental.pallas import tpu as pltpu
from jax.sharding import PartitionSpec as P

MESH = pl.DeviceIdType.MESH
F32, BF16 = jnp.float32, jnp.bfloat16
LATENT, ROPE, VALUE = 512, 64, 128
FEAT = LATENT + ROPE
WIDE = 640
TOK = 128
HEADS = 16
ROWS = TOK * HEADS
CHUNK = 2 * TOK
NCH = 9
SHARD = 32
DIRECT = (1, 3)
ALONG = (5, 7)
SHARDS = (1, 3, 2, 6, 5, 7)
YFIRST = 6
RB = 1024
STEPS = ((0,), (4,), (8, 1), (3, 2), (6, 5, 7))
C = 192.0 ** -0.5 * 1.4426950408889634
BIG = -1.0e30
NT = (((1,), (1,)), ((), ()))


def kernel(q_hbm, lat_hbm, seg_hbm, w_hbm, o_ref,
           lat_ref, seg_ref, in_sem, kbuf, wbuf, qv, qs, segc, S, mx, lsum, top, acc, ctx,
           q_sem, w_sem, sx, rx, sb, sy, ry, sz, rz, ss, rs, swy, rwy, swz, rwz, sws, rws):
    dp, tp = lax.axis_index("dp"), lax.axis_index("tp")
    core = lax.rem(dp, 2)
    y = lax.rem(dp // 2, 4)
    z = dp // 8
    sib = dp + 1 - 2 * core

    def xpeer(d):
        return (dp, lax.rem(tp + d, 4))

    def ypeer(d):
        return (z * 8 + lax.rem(y + d, 4) * 2 + core, tp)

    def zpeer(d):
        return (lax.rem(z + d, 4) * 8 + y * 2 + core, tp)

    def has_src(k):
        return dp - 2 * k >= 0

    icopy = [pltpu.make_async_copy(lat_hbm, lat_ref, in_sem.at[0]), pltpu.make_async_copy(seg_hbm, seg_ref, in_sem.at[1])]
    for cp in icopy:
        cp.start()
    qcopy = [pltpu.make_async_copy(q_hbm.at[:, pl.ds(g * 2 * FEAT, 2 * FEAT)], qv.at[g], q_sem.at[g]) for g in range(HEADS // 2)]
    for cp in qcopy:
        cp.start()
    wown = pltpu.make_async_copy(w_hbm, wbuf.at[:, z, y, core], w_sem.at[0])
    wown.start()

    barrier = pltpu.get_barrier_semaphore()

    def greet(dev):
        pl.semaphore_signal(barrier, inc=1, device_id=dev, device_id_type=MESH)

    for d in range(1, 4):
        greet(xpeer(d))
        greet(ypeer(d))
        greet(zpeer(d))
    greet((sib, tp))
    for k in DIRECT:
        @pl.when((core == 0) & has_src(k))
        def _():
            greet((dp - 2 * k, tp))

    for cp in icopy:
        cp.wait()
    seg = jnp.broadcast_to(seg_ref[...].astype(F32), (TOK, TOK))
    segc[...] = jnp.transpose(seg)
    my_rows = pl.ds(pl.multiple_of(core * TOK + tp * SHARD, SHARD), SHARD)
    half = pl.ds(pl.multiple_of(core * TOK, TOK), TOK)
    other = pl.ds(pl.multiple_of((1 - core) * TOK, TOK), TOK)
    lane32 = lax.broadcasted_iota(jnp.int32, (SHARD, 128), 1).astype(F32)
    mine = segc[pl.ds(pl.multiple_of(tp * SHARD, SHARD), SHARD), :]
    kfeat = jnp.where((lane32 >= 4.0) | (lane32 == mine), 0.0, BIG).astype(BF16)
    kbuf[0, my_rows, 0:FEAT] = lat_ref[...]
    kbuf[0, my_rows, FEAT:WIDE] = kfeat[:, :WIDE - FEAT]

    n_wait = 10 + jnp.where(core == 0, jnp.where(dp + 2 <= 31, 1, 0) + jnp.where(dp + 6 <= 31, 1, 0), 0)
    pl.semaphore_wait(barrier, n_wait)

    def remote(ref, dst, ssem, rsem, dev):
        return pltpu.make_async_remote_copy(ref, dst, ssem, rsem, device_id=dev, device_id_type=MESH)

    def zdev(v):
        return (v * 8 + y * 2 + core, tp)

    def xcopy(k, d):
        at = kbuf.at[k, my_rows, :]
        return remote(at, at, sx.at[k], rx.at[k], xpeer(d))

    def xthree(k):
        at = kbuf.at[k, pl.ds(0, 3 * SHARD), :]
        return remote(at, at, sx.at[k], rx.at[k], xpeer(1))

    def zcopy(r):
        return remote(kbuf.at[0, my_rows, :], kbuf.at[4 * r, my_rows, :], sz.at[r], rz.at[r], zdev(lax.rem(z + r, 4)))

    first = core == 0
    second = core == 1

    def yrow(k):
        return k // 4 + jnp.where(y + k % 4 <= 3, 0, 1)

    def ycopy(k, rows):
        return remote(kbuf.at[4 * yrow(k), rows, :], kbuf.at[k, rows, :], sy.at[k], ry.at[k], ypeer(k % 4))

    def yneed(k):
        return z >= yrow(k)

    def bcopy(k):
        return remote(kbuf.at[0, half, :], kbuf.at[k, half, :], sb.at[k], ry.at[k], (dp + 2 * k, tp))

    def scopy(k):
        at = kbuf.at[k, half, :]
        return remote(at, at, ss.at[k], rs.at[k], (sib, tp))


    lo, hi = pl.ds(0, YFIRST), pl.ds(YFIRST, HEADS - YFIRST)

    def wy1(d):
        return remote(w_hbm.at[lo], wbuf.at[lo, z, y, core], swy.at[0], rwy.at[0], ypeer(d))

    def wz1(d):
        return remote(w_hbm.at[hi], wbuf.at[hi, z, y, core], swz.at[0], rwz.at[0], zpeer(d))

    def wz2(d):
        at = wbuf.at[lo, z, :, core]
        return remote(at, at, swz.at[1], rwz.at[1], zpeer(d))

    def wy2(d):
        at = wbuf.at[hi, :, y, core]
        return remote(at, at, swy.at[1], rwy.at[1], ypeer(d))

    def wthree(along_y, stage):
        heads = lo if along_y == (stage == 0) else hi
        at = wbuf.at[heads, pl.ds(0, 3), 0, 0] if stage == 0 else wbuf.at[heads, pl.ds(0, 3), :, 0]
        if along_y:
            return remote(at, at, swy.at[stage], rwy.at[stage], ypeer(1))
        return remote(at, at, swz.at[stage], rwz.at[stage], zpeer(1))

    def wsib(i):
        at = wbuf.at[(lo, hi)[i], :, :, core]
        return remote(at, at, sws.at[i], rws.at[i], (sib, tp))

    def shards(k):
        return second if k in DIRECT + ALONG else True

    for r in (1, 2):
        @pl.when(z + r <= 3)
        def _():
            zcopy(r).start()
    for d in (1, 3, 2):
        xcopy(0, d).start()
    for k in SHARDS:
        @pl.when((yrow(k) == 0) & shards(k))
        def _():
            ycopy(k, my_rows).start()

    segv = segc[...]
    lane = lax.broadcasted_iota(jnp.int32, (TOK, 128), 1)
    onehot = jnp.where((lane - 64).astype(F32) == segv, 1.0, 0.0)

    def prep(g):
        qcopy[g].wait()
        even = qv[g, :, 0:WIDE]
        odd = pltpu.roll(qv[g, :, LATENT:2 * FEAT], WIDE - 64, 1)
        for i, v in ((0, even), (1, odd)):
            r = pl.ds((2 * g + i) * TOK, TOK)
            qs[r, 0:LATENT] = v[:, 0:LATENT]
            qs[r, LATENT:WIDE] = jnp.where(lane < 64, v[:, LATENT:WIDE].astype(F32), onehot).astype(BF16)

    for k in range(1, NCH):
        @pl.when(jnp.logical_not(has_src(k)))
        def _():
            ln = lax.broadcasted_iota(jnp.int32, (CHUNK, 128), 1)
            kbuf[k, :, 0:LATENT] = jnp.zeros((CHUNK, LATENT), BF16)
            kbuf[k, :, LATENT:WIDE] = jnp.where((ln >= 64) & (ln < 68), BIG, 0.0).astype(BF16)

    for g in range(HEADS // 2):
        prep(g)

    for r in (1, 2):
        @pl.when(z >= r)
        def _():
            zcopy(r).wait_recv()
            for d in (1, 3, 2):
                xcopy(4 * r, d).start()
        for k in SHARDS:
            @pl.when(yneed(k) & (yrow(k) == r) & shards(k))
            def _():
                ycopy(k, my_rows).start()
    for d in (1, 3, 2):
        wz1(d).start()
        wy1(d).start()
    xthree(0).wait_recv()
    scopy(0).start()
    for k in DIRECT:
        @pl.when(first & (dp + 2 * k <= 31))
        def _():
            bcopy(k).start()
    def issue(k):
        @pl.when(shards(k) & has_src(k))
        def _():
            ycopy(k, my_rows).wait_recv()
            for d in (1, 3, 2):
                xcopy(k, d).start()

    def along(k, r):
        @pl.when(first & yneed(k) & (yrow(k) == r))
        def _():
            ycopy(k, half).start()

    def weights2():
        wown.wait()
        wthree(False, 0).wait_recv()
        for d in (1, 3, 2):
            wy2(d).start()
        wthree(True, 0).wait_recv()
        for d in (1, 3, 2):
            wz2(d).start()

    def weights4():
        wthree(False, 1).wait_recv()
        wsib(0).start()

    def weights5():
        wthree(True, 1).wait_recv()
        wsib(1).start()

    def relay(k, who=None):
        if k in DIRECT + ALONG:
            @pl.when(first & has_src(k))
            def _():
                (bcopy(k) if k in DIRECT else ycopy(k, half)).wait_recv()
                scopy(k).start()

        mine = shards(k) if who is None else who

        @pl.when(has_src(k) & mine)
        def _():
            xthree(k).wait_recv()
            scopy(k).start()

    def arrive(k):
        if k == 0:
            scopy(0).wait_recv()
        else:
            @pl.when(has_src(k))
            def _():
                scopy(k).wait_recv()

    def score(ks, slot, r):
        rows = pl.ds(r * RB, RB)
        best = None
        for j, k in enumerate(ks):
            s = lax.dot_general(qs[rows, :], kbuf[k], NT, preferred_element_type=F32)
            if k == 0:
                rr = lax.broadcasted_iota(jnp.int32, (RB, CHUNK), 0)
                cc = lax.broadcasted_iota(jnp.int32, (RB, CHUNK), 1)
                s = jnp.where(cc <= (rr & (TOK - 1)) + core * TOK, s, BIG)
            S[slot, j, rows, :] = s
            m = jnp.maximum(s[:, :128], s[:, 128:])
            best = m if best is None else jnp.maximum(best, m)
        mx[slot, rows, :] = best

    def values(ks, slot, r, begin, last):
        rows = pl.ds(r * RB, RB)
        m = jnp.max(mx[slot, rows, :], axis=1, keepdims=True) * C
        if not begin:
            m = jnp.maximum(m, top[rows, 0:1])
        l, ps = None, []
        for j in range(len(ks)):
            p = jnp.exp2(S[slot, j, rows, :] * C - m)
            t = p[:, :128] + p[:, 128:]
            l = t if l is None else l + t
            ps.append(p.astype(BF16))
        p = jnp.concatenate(ps, axis=1) if len(ks) > 1 else ps[0]
        v = jnp.concatenate([kbuf[k, :, 0:LATENT] for k in ks], axis=0)
        a = jnp.dot(p, v, preferred_element_type=F32)
        if not begin:
            al = jnp.exp2(top[rows, 0:1] - m)
            a = a + acc[rows, :] * al
            l = l + lsum[rows, :] * al
        if last:
            inv = 1.0 / jnp.sum(l, axis=1, keepdims=True)
            ctx[rows, :] = (a * inv).astype(BF16)
        else:
            acc[rows, :] = a
            lsum[rows, :] = l
            top[rows, :] = jnp.broadcast_to(m, (RB, 128))

    def step(i):
        for r in range(ROWS // RB):
            if i < len(STEPS):
                score(STEPS[i], i % 2, r)
            if i > 0:
                values(STEPS[i - 1], (i - 1) % 2, r, i == 1, i == len(STEPS))

    def early():
        xthree(0).wait_send()
        scopy(0).wait_send()
        wthree(True, 0).wait_send()
        wthree(False, 0).wait_send()
        for r in (1, 2):
            @pl.when(z + r <= 3)
            def _():
                zcopy(r).wait_send()

            @pl.when(z >= r)
            def _():
                xthree(4 * r).wait_send()
                scopy(4 * r).wait_send()
        for k in SHARDS:
            @pl.when(yneed(k) & shards(k))
            def _():
                ycopy(k, my_rows).wait_send()
        for k in DIRECT:
            @pl.when(first & (dp + 2 * k <= 31))
            def _():
                bcopy(k).wait_send()

    issue(1)
    arrive(0)
    step(0)
    issue(3)
    issue(2)
    issue(6)
    issue(5)
    issue(7)
    relay(4)
    along(5, 1)
    along(7, 1)
    relay(8)
    along(5, 2)
    along(7, 2)
    weights2()
    arrive(4)
    step(1)
    relay(1)
    relay(3)
    relay(2, second)
    arrive(8)
    arrive(1)
    step(2)
    relay(2, first)
    relay(6)
    early()
    relay(5)
    relay(7)
    arrive(3)
    arrive(2)
    step(3)
    weights4()
    weights5()
    arrive(6)
    arrive(5)
    arrive(7)
    step(4)
    wsib(0).wait_recv()
    wsib(1).wait_recv()
    step(len(STEPS))
    for h in range(HEADS):
        wv = wbuf[h].reshape(LATENT, VALUE)
        o_ref[:, h * VALUE:(h + 1) * VALUE] = jnp.dot(ctx[h * TOK:(h + 1) * TOK, :], wv, preferred_element_type=F32).astype(BF16)
    wthree(True, 1).wait_send()
    wthree(False, 1).wait_send()
    wsib(0).wait_send()
    wsib(1).wait_send()
    for k in ALONG:
        @pl.when(first & yneed(k))
        def _():
            ycopy(k, half).wait_send()
    for k in SHARDS:
        @pl.when(has_src(k))
        def _():
            scopy(k).wait_send()

        @pl.when(has_src(k) & shards(k))
        def _():
            xthree(k).wait_send()


def per_device(queries, latents, segment_ids, value_weight):
    dma = pltpu.SemaphoreType.DMA
    return pl.pallas_call(
        kernel,
        out_shape=pltpu.VMEM((TOK, HEADS * VALUE), BF16),
        in_specs=[pl.BlockSpec(memory_space=pltpu.HBM)] * 4,
        out_specs=pl.BlockSpec(memory_space=pltpu.VMEM),
        scratch_shapes=[
            pltpu.VMEM((SHARD, FEAT), BF16), pltpu.VMEM((1, TOK), jnp.int32), dma((2,)),
            pltpu.VMEM((NCH, CHUNK, WIDE), BF16),
            pltpu.VMEM((HEADS, 4, 4, 2, 16, VALUE), BF16),
            pltpu.VMEM((HEADS // 2, TOK, 2 * FEAT), BF16),
            pltpu.VMEM((ROWS, WIDE), BF16),
            pltpu.VMEM((TOK, 128), F32),
            pltpu.VMEM((2, max(len(g) for g in STEPS), ROWS, CHUNK), F32),
            pltpu.VMEM((2, ROWS, 128), F32),
            pltpu.VMEM((ROWS, 128), F32),
            pltpu.VMEM((ROWS, 128), F32),
            pltpu.VMEM((ROWS, LATENT), F32),
            pltpu.VMEM((ROWS, LATENT), BF16),
            dma((HEADS // 2,)), dma((1,)),
            dma((NCH,)), dma((NCH,)),
            dma((NCH,)), dma((NCH,)), dma((NCH,)),
            dma((3,)), dma((3,)),
            dma((NCH,)), dma((NCH,)),
            dma((2,)), dma((2,)),
            dma((2,)), dma((2,)),
            dma((2,)), dma((2,)),
        ],
        compiler_params=pltpu.CompilerParams(collective_id=0, has_side_effects=True, vmem_limit_bytes=48 * 2 ** 20),
        cost_estimate=pl.CostEstimate(flops=11 * 10 ** 9, bytes_accessed=8 * 10 ** 6, transcendentals=5 * 10 ** 6),
    )(*[pltpu.with_memory_space_constraint(x, pltpu.HBM) for x in (queries, latents, segment_ids.reshape(1, TOK), value_weight)])


def solution(mesh):
    placed = (P("dp", "tp"), P(("dp", "tp"), None), P("dp"), P("tp", "dp", None))
    return jax.shard_map(per_device, mesh=mesh, in_specs=placed, out_specs=P("dp", "tp"), check_vma=False)
```

```python
import functools

import jax
import jax.numpy as jnp
from jax import lax
from jax.experimental import pallas as pl
from jax.experimental.pallas import tpu as pltpu
from jax.sharding import PartitionSpec as P

MESH = pl.DeviceIdType.MESH
F32, BF16 = jnp.float32, jnp.bfloat16
LATENT, ROPE, VALUE = 512, 64, 128
FEAT = LATENT + ROPE
WIDE = 640
TOK = 128
HEADS = 16
ROWS = TOK * HEADS
CHUNK = 2 * TOK
NCH = 9
SHARD = 32
DIRECT = (1, 3)
ALONG = (5, 7)
SHARDS = (1, 3, 2, 6, 5, 7)
YFIRST = 6
RB = 1024
STEPS = ((0,), (4,), (8, 1), (3, 2), (6, 5, 7))
C = 192.0 ** -0.5 * 1.4426950408889634
BIG = -1.0e30
NT = (((1,), (1,)), ((), ()))


def kernel(q_hbm, lat_hbm, seg_hbm, w_hbm, o_ref,
           lat_ref, seg_ref, in_sem, kbuf, wbuf, qv, qs, segc, S, mx, lsum, top, acc, ctx,
           q_sem, w_sem, sx, rx, sb, sy, ry, sz, rz, ss, rs, swy, rwy, swz, rwz, sws, rws):
    dp, tp = lax.axis_index("dp"), lax.axis_index("tp")
    core = lax.rem(dp, 2)
    y = lax.rem(dp // 2, 4)
    z = dp // 8
    sib = dp + 1 - 2 * core

    def xpeer(d):
        return (dp, lax.rem(tp + d, 4))

    def ypeer(d):
        return (z * 8 + lax.rem(y + d, 4) * 2 + core, tp)

    def zpeer(d):
        return (lax.rem(z + d, 4) * 8 + y * 2 + core, tp)

    def has_src(k):
        return dp - 2 * k >= 0

    icopy = [pltpu.make_async_copy(lat_hbm, lat_ref, in_sem.at[0]), pltpu.make_async_copy(seg_hbm, seg_ref, in_sem.at[1])]
    for cp in icopy:
        cp.start()
    qcopy = [pltpu.make_async_copy(q_hbm.at[:, pl.ds(g * 2 * FEAT, 2 * FEAT)], qv.at[g], q_sem.at[g]) for g in range(HEADS // 2)]
    for cp in qcopy:
        cp.start()
    wown = pltpu.make_async_copy(w_hbm, wbuf.at[:, z, y, core], w_sem.at[0])
    wown.start()

    barrier = pltpu.get_barrier_semaphore()

    def greet(dev):
        pl.semaphore_signal(barrier, inc=1, device_id=dev, device_id_type=MESH)

    for d in range(1, 4):
        greet(xpeer(d))
        greet(ypeer(d))
        greet(zpeer(d))
    greet((sib, tp))
    for k in DIRECT:
        @pl.when((core == 0) & has_src(k))
        def _():
            greet((dp - 2 * k, tp))

    for cp in icopy:
        cp.wait()
    seg = jnp.broadcast_to(seg_ref[...].astype(F32), (TOK, TOK))
    segc[...] = jnp.transpose(seg)
    my_rows = pl.ds(pl.multiple_of(core * TOK + tp * SHARD, SHARD), SHARD)
    half = pl.ds(pl.multiple_of(core * TOK, TOK), TOK)
    other = pl.ds(pl.multiple_of((1 - core) * TOK, TOK), TOK)
    lane32 = lax.broadcasted_iota(jnp.int32, (SHARD, 128), 1).astype(F32)
    mine = segc[pl.ds(pl.multiple_of(tp * SHARD, SHARD), SHARD), :]
    kfeat = jnp.where((lane32 >= 4.0) | (lane32 == mine), 0.0, BIG).astype(BF16)
    kbuf[0, my_rows, 0:FEAT] = lat_ref[...]
    kbuf[0, my_rows, FEAT:WIDE] = kfeat[:, :WIDE - FEAT]

    n_wait = 10 + jnp.where(core == 0, jnp.where(dp + 2 <= 31, 1, 0) + jnp.where(dp + 6 <= 31, 1, 0), 0)
    pl.semaphore_wait(barrier, n_wait)

    def remote(ref, dst, ssem, rsem, dev):
        return pltpu.make_async_remote_copy(ref, dst, ssem, rsem, device_id=dev, device_id_type=MESH)

    def zdev(v):
        return (v * 8 + y * 2 + core, tp)

    def xcopy(k, d):
        at = kbuf.at[k, my_rows, :]
        return remote(at, at, sx.at[k], rx.at[k], xpeer(d))

    def xthree(k):
        at = kbuf.at[k, pl.ds(0, 3 * SHARD), :]
        return remote(at, at, sx.at[k], rx.at[k], xpeer(1))

    def zcopy(r):
        return remote(kbuf.at[0, my_rows, :], kbuf.at[4 * r, my_rows, :], sz.at[r], rz.at[r], zdev(lax.rem(z + r, 4)))

    first = core == 0
    second = core == 1

    def yrow(k):
        return k // 4 + jnp.where(y + k % 4 <= 3, 0, 1)

    def ycopy(k, rows):
        return remote(kbuf.at[4 * yrow(k), rows, :], kbuf.at[k, rows, :], sy.at[k], ry.at[k], ypeer(k % 4))

    def yneed(k):
        return z >= yrow(k)

    def bcopy(k):
        return remote(kbuf.at[0, half, :], kbuf.at[k, half, :], sb.at[k], ry.at[k], (dp + 2 * k, tp))

    def scopy(k):
        at = kbuf.at[k, half, :]
        return remote(at, at, ss.at[k], rs.at[k], (sib, tp))


    lo, hi = pl.ds(0, YFIRST), pl.ds(YFIRST, HEADS - YFIRST)

    def wy1(d):
        return remote(w_hbm.at[lo], wbuf.at[lo, z, y, core], swy.at[0], rwy.at[0], ypeer(d))

    def wz1(d):
        return remote(w_hbm.at[hi], wbuf.at[hi, z, y, core], swz.at[0], rwz.at[0], zpeer(d))

    def wz2(d):
        at = wbuf.at[lo, z, :, core]
        return remote(at, at, swz.at[1], rwz.at[1], zpeer(d))

    def wy2(d):
        at = wbuf.at[hi, :, y, core]
        return remote(at, at, swy.at[1], rwy.at[1], ypeer(d))

    def wthree(along_y, stage):
        heads = lo if along_y == (stage == 0) else hi
        at = wbuf.at[heads, pl.ds(0, 3), 0, 0] if stage == 0 else wbuf.at[heads, pl.ds(0, 3), :, 0]
        if along_y:
            return remote(at, at, swy.at[stage], rwy.at[stage], ypeer(1))
        return remote(at, at, swz.at[stage], rwz.at[stage], zpeer(1))

    def wsib(i):
        at = wbuf.at[(lo, hi)[i], :, :, core]
        return remote(at, at, sws.at[i], rws.at[i], (sib, tp))

    def shards(k):
        return second if k in DIRECT + ALONG else True

    for r in (1, 2):
        @pl.when(z + r <= 3)
        def _():
            zcopy(r).start()
    for d in (1, 3, 2):
        xcopy(0, d).start()
    for k in SHARDS:
        @pl.when((yrow(k) == 0) & shards(k))
        def _():
            ycopy(k, my_rows).start()

    segv = segc[...]
    lane = lax.broadcasted_iota(jnp.int32, (TOK, 128), 1)
    onehot = jnp.where((lane - 64).astype(F32) == segv, 1.0, 0.0)

    def prep(g):
        qcopy[g].wait()
        even = qv[g, :, 0:WIDE]
        odd = pltpu.roll(qv[g, :, LATENT:2 * FEAT], WIDE - 64, 1)
        for i, v in ((0, even), (1, odd)):
            r = pl.ds((2 * g + i) * TOK, TOK)
            qs[r, 0:LATENT] = v[:, 0:LATENT]
            qs[r, LATENT:WIDE] = jnp.where(lane < 64, v[:, LATENT:WIDE].astype(F32), onehot).astype(BF16)

    for k in range(1, NCH):
        @pl.when(jnp.logical_not(has_src(k)))
        def _():
            ln = lax.broadcasted_iota(jnp.int32, (CHUNK, 128), 1)
            kbuf[k, :, 0:LATENT] = jnp.zeros((CHUNK, LATENT), BF16)
            kbuf[k, :, LATENT:WIDE] = jnp.where((ln >= 64) & (ln < 68), BIG, 0.0).astype(BF16)

    for g in range(HEADS // 2):
        prep(g)

    for r in (1, 2):
        @pl.when(z >= r)
        def _():
            zcopy(r).wait_recv()
            for d in (1, 3, 2):
                xcopy(4 * r, d).start()
        for k in SHARDS:
            @pl.when(yneed(k) & (yrow(k) == r) & shards(k))
            def _():
                ycopy(k, my_rows).start()
    for d in (1, 3, 2):
        wz1(d).start()
        wy1(d).start()
    xthree(0).wait_recv()
    scopy(0).start()
    for k in DIRECT:
        @pl.when(first & (dp + 2 * k <= 31))
        def _():
            bcopy(k).start()
    def issue(k):
        @pl.when(shards(k) & has_src(k))
        def _():
            ycopy(k, my_rows).wait_recv()
            for d in (1, 3, 2):
                xcopy(k, d).start()

    def along(k, r):
        @pl.when(first & yneed(k) & (yrow(k) == r))
        def _():
            ycopy(k, half).start()

    def weights2():
        wown.wait()
        wthree(False, 0).wait_recv()
        for d in (2, 1, 3):
            wy2(d).start()
        wthree(True, 0).wait_recv()
        for d in (1, 3, 2):
            wz2(d).start()

    def weights4():
        wthree(False, 1).wait_recv()
        wsib(0).start()

    def weights5():
        wthree(True, 1).wait_recv()
        wsib(1).start()

    def relay(k, who=None):
        if k in DIRECT + ALONG:
            @pl.when(first & has_src(k))
            def _():
                (bcopy(k) if k in DIRECT else ycopy(k, half)).wait_recv()
                scopy(k).start()

        mine = shards(k) if who is None else who

        @pl.when(has_src(k) & mine)
        def _():
            xthree(k).wait_recv()
            scopy(k).start()

    def arrive(k):
        if k == 0:
            scopy(0).wait_recv()
        else:
            @pl.when(has_src(k))
            def _():
                scopy(k).wait_recv()

    def score(ks, slot, r):
        rows = pl.ds(r * RB, RB)
        best = None
        for j, k in enumerate(ks):
            s = lax.dot_general(qs[rows, :], kbuf[k], NT, preferred_element_type=F32)
            if k == 0:
                rr = lax.broadcasted_iota(jnp.int32, (RB, CHUNK), 0)
                cc = lax.broadcasted_iota(jnp.int32, (RB, CHUNK), 1)
                s = jnp.where(cc <= (rr & (TOK - 1)) + core * TOK, s, BIG)
            S[slot, j, rows, :] = s
            m = jnp.maximum(s[:, :128], s[:, 128:])
            best = m if best is None else jnp.maximum(best, m)
        mx[slot, rows, :] = best

    def values(ks, slot, r, begin, last):
        rows = pl.ds(r * RB, RB)
        m = jnp.max(mx[slot, rows, :], axis=1, keepdims=True) * C
        if not begin:
            m = jnp.maximum(m, top[rows, 0:1])
        l, ps = None, []
        for j in range(len(ks)):
            p = jnp.exp2(S[slot, j, rows, :] * C - m)
            t = p[:, :128] + p[:, 128:]
            l = t if l is None else l + t
            ps.append(p.astype(BF16))
        p = jnp.concatenate(ps, axis=1) if len(ks) > 1 else ps[0]
        v = jnp.concatenate([kbuf[k, :, 0:LATENT] for k in ks], axis=0)
        a = jnp.dot(p, v, preferred_element_type=F32)
        if not begin:
            al = jnp.exp2(top[rows, 0:1] - m)
            a = a + acc[rows, :] * al
            l = l + lsum[rows, :] * al
        if last:
            inv = 1.0 / jnp.sum(l, axis=1, keepdims=True)
            ctx[rows, :] = (a * inv).astype(BF16)
        else:
            acc[rows, :] = a
            lsum[rows, :] = l
            top[rows, :] = jnp.broadcast_to(m, (RB, 128))

    def step(i):
        for r in range(ROWS // RB):
            if i < len(STEPS):
                score(STEPS[i], i % 2, r)
            if i > 0:
                values(STEPS[i - 1], (i - 1) % 2, r, i == 1, i == len(STEPS))

    def early():
        xthree(0).wait_send()
        scopy(0).wait_send()
        wthree(True, 0).wait_send()
        wthree(False, 0).wait_send()
        for r in (1, 2):
            @pl.when(z + r <= 3)
            def _():
                zcopy(r).wait_send()

            @pl.when(z >= r)
            def _():
                xthree(4 * r).wait_send()
                scopy(4 * r).wait_send()
        for k in SHARDS:
            @pl.when(yneed(k) & shards(k))
            def _():
                ycopy(k, my_rows).wait_send()
        for k in DIRECT:
            @pl.when(first & (dp + 2 * k <= 31))
            def _():
                bcopy(k).wait_send()

    issue(1)
    arrive(0)
    step(0)
    issue(3)
    issue(2)
    issue(6)
    issue(5)
    issue(7)
    relay(4)
    along(5, 1)
    along(7, 1)
    relay(8)
    along(5, 2)
    along(7, 2)
    weights2()
    arrive(4)
    step(1)
    relay(1)
    relay(3)
    relay(2, second)
    arrive(8)
    arrive(1)
    step(2)
    relay(2, first)
    relay(6)
    early()
    relay(5)
    relay(7)
    arrive(3)
    arrive(2)
    step(3)
    weights4()
    weights5()
    arrive(6)
    arrive(5)
    arrive(7)
    step(4)
    wsib(0).wait_recv()
    wsib(1).wait_recv()
    step(len(STEPS))
    for h in range(HEADS):
        wv = wbuf[h].reshape(LATENT, VALUE)
        o_ref[:, h * VALUE:(h + 1) * VALUE] = jnp.dot(ctx[h * TOK:(h + 1) * TOK, :], wv, preferred_element_type=F32).astype(BF16)
    wthree(True, 1).wait_send()
    wthree(False, 1).wait_send()
    wsib(0).wait_send()
    wsib(1).wait_send()
    for k in ALONG:
        @pl.when(first & yneed(k))
        def _():
            ycopy(k, half).wait_send()
    for k in SHARDS:
        @pl.when(has_src(k))
        def _():
            scopy(k).wait_send()

        @pl.when(has_src(k) & shards(k))
        def _():
            xthree(k).wait_send()


def per_device(queries, latents, segment_ids, value_weight):
    dma = pltpu.SemaphoreType.DMA
    return pl.pallas_call(
        kernel,
        out_shape=pltpu.VMEM((TOK, HEADS * VALUE), BF16),
        in_specs=[pl.BlockSpec(memory_space=pltpu.HBM)] * 4,
        out_specs=pl.BlockSpec(memory_space=pltpu.VMEM),
        scratch_shapes=[
            pltpu.VMEM((SHARD, FEAT), BF16), pltpu.VMEM((1, TOK), jnp.int32), dma((2,)),
            pltpu.VMEM((NCH, CHUNK, WIDE), BF16),
            pltpu.VMEM((HEADS, 4, 4, 2, 16, VALUE), BF16),
            pltpu.VMEM((HEADS // 2, TOK, 2 * FEAT), BF16),
            pltpu.VMEM((ROWS, WIDE), BF16),
            pltpu.VMEM((TOK, 128), F32),
            pltpu.VMEM((2, max(len(g) for g in STEPS), ROWS, CHUNK), F32),
            pltpu.VMEM((2, ROWS, 128), F32),
            pltpu.VMEM((ROWS, 128), F32),
            pltpu.VMEM((ROWS, 128), F32),
            pltpu.VMEM((ROWS, LATENT), F32),
            pltpu.VMEM((ROWS, LATENT), BF16),
            dma((HEADS // 2,)), dma((1,)),
            dma((NCH,)), dma((NCH,)),
            dma((NCH,)), dma((NCH,)), dma((NCH,)),
            dma((3,)), dma((3,)),
            dma((NCH,)), dma((NCH,)),
            dma((2,)), dma((2,)),
            dma((2,)), dma((2,)),
            dma((2,)), dma((2,)),
        ],
        compiler_params=pltpu.CompilerParams(collective_id=0, has_side_effects=True, vmem_limit_bytes=48 * 2 ** 20),
        cost_estimate=pl.CostEstimate(flops=11 * 10 ** 9, bytes_accessed=8 * 10 ** 6, transcendentals=5 * 10 ** 6),
    )(*[pltpu.with_memory_space_constraint(x, pltpu.HBM) for x in (queries, latents, segment_ids.reshape(1, TOK), value_weight)])


def solution(mesh):
    placed = (P("dp", "tp"), P(("dp", "tp"), None), P("dp"), P("tp", "dp", None))
    return jax.shard_map(per_device, mesh=mesh, in_specs=placed, out_specs=P("dp", "tp"), check_vma=False)
```
